128 devices in a mesh: seq: 32 (over z, x, core), batch: 4 (over y).
Axes of the slice: x: 4, y: 4, z: 4, core: 2. Of those that a mesh axis runs over, the one named last changes fastest.
Arguments:
- queries: bfloat16 [512, 4096], P(('batch', 'seq')), parts along dimension 0, may hold values from -720 to 720
- prompt_keys: bfloat16 [131072, 512], P(('batch', 'seq')), parts along dimension 0, may hold values from -6 to 6
- prompt_values: bfloat16 [131072, 512], P(('batch', 'seq')), parts along dimension 0, may hold values from -12 to 12
- response_keys: bfloat16 [512, 512], P(('batch', 'seq')), parts along dimension 0, may hold values from -6 to 6
- response_values: bfloat16 [512, 512], P(('batch', 'seq')), parts along dimension 0, may hold values from -12 to 12
- resp_len: int32 [4], P('batch'), parts along dimension 0, may hold values from 32 to 128
- residual: bfloat16 [512, 4096], P('batch', 'seq'), parts along dimension 0, may hold values from -6 to 6
- out_weight: bfloat16 [4096, 4096], P(None, 'seq'), may hold values from -0.09375 to 0.09375
- norm_gain: float32 [4096], P('seq'), may hold values from 0.5 to 40
- vocab_weight: bfloat16 [4096, 77824], P(None, 'seq'), may hold values from -0.25 to 0.25
- targets: int32 [512], P('batch'), parts along dimension 0, may hold values from 0 to 77823
Outputs:
- layer_out: bfloat16 [512, 4096], P('batch', 'seq'), parts along dimension 0
- row_loss: float32 [512], P('batch'), parts along dimension 0
The draws below stay inside these ranges and needn't reach their ends.
There are 4 independent parts, one for each index of `batch`. The reference program is written for one: setup_inputs(seed, part) draws one part's arguments, and reference() takes and returns one part's arrays. A program takes and returns all parts, laid end to end along the dimension named above; an argument that names none is the same for every part. Nothing has to cross between parts.
All inputs are finite; a program needn't handle non-finite values.
Results may differ from the reference program's by a relative error of at most 0.01525.
Values may be sent and summed in bfloat16 or wider, within the bound.
A program may use at most 192 MiB of HBM per device.

```python
import math
import jax
import jax.numpy as jnp
from jax import lax

D = 4096
QUERY_HEADS = 32
KEY_VALUE_HEADS = 4
HEAD_SIZE = 128
VOCAB = 77824
PROMPT_TOKENS = 32768
RESPONSE_ROWS = 128


def draw_queries(key, part):
    key = jax.random.fold_in(key, 11)
    base = jnp.clip(jax.random.normal(key, (RESPONSE_ROWS, QUERY_HEADS * HEAD_SIZE), jnp.float32), -6.0, 6.0) * 3.0
    return base.astype(jnp.bfloat16)


def draw_residual(key, part):
    key = jax.random.fold_in(key, 23)
    columns = jnp.arange(D, dtype=jnp.float32) / (D - 1)
    scale = 0.1 * jnp.exp(columns * math.log(10.0))
    base = jnp.clip(jax.random.normal(key, (RESPONSE_ROWS, D), jnp.float32), -6.0, 6.0)
    return (base * scale[None, :]).astype(jnp.bfloat16)


def draw_norm_gain(key, part):
    key = jax.random.fold_in(key, 37)
    gain = 1.0 + 0.1 * jnp.clip(jax.random.normal(key, (D,), jnp.float32), -5.0, 5.0)
    return gain


def touch_ends(values, rng, low, largest):
    extent = values.shape
    index_at = [jax.random.randint(jax.random.fold_in(rng, axis), (), 0, extent[axis]) for axis in range(len(extent))]
    values = values.at[tuple(index_at)].set(low)
    longest = extent.index(max(extent))
    index_at[longest] = (index_at[longest] + 1) % extent[longest]
    return values.at[tuple(index_at)].set(largest)


def shard_levels(key, dims, pieces, low, largest):
    level = 1.0
    for axis_at, shards_of in pieces:
        draws = jax.random.uniform(jax.random.fold_in(jax.random.fold_in(key, 6), axis_at), (shards_of,), jnp.float32, low / len(pieces), largest / len(pieces))
        level = level * jnp.repeat(jnp.exp(draws), dims[axis_at] // shards_of).reshape((-1,) + (1,) * (len(dims) - 1 - axis_at))
    return level


def noise(own_key, dims, scale, bound, split=(), held_as=jnp.bfloat16):
    array = scale * jax.random.normal(own_key, dims, jnp.float32)
    if split:
        array = array * shard_levels(own_key, dims, split, -0.22, 0.18)
    return jnp.clip(array, -bound, bound).astype(held_as)


def setup_inputs(seed: int = 0, part: int = 0) -> dict:
    arg_keys = jax.random.split(jax.random.key(seed), 12)
    part_keys = jax.random.split(jax.random.fold_in(arg_keys[11], part), 12)
    return {
        "queries": draw_queries(jax.random.fold_in(jax.random.fold_in(arg_keys[11], part), 71), part),
        "prompt_keys": noise(part_keys[1], (PROMPT_TOKENS, KEY_VALUE_HEADS * HEAD_SIZE), 1.0, 6.0, ((0, 32),)),
        "prompt_values": noise(part_keys[2], (PROMPT_TOKENS, KEY_VALUE_HEADS * HEAD_SIZE), 2.0, 12.0, ((0, 32),)),
        "response_keys": noise(part_keys[3], (RESPONSE_ROWS, KEY_VALUE_HEADS * HEAD_SIZE), 1.0, 6.0, ((0, 32),)),
        "response_values": noise(part_keys[4], (RESPONSE_ROWS, KEY_VALUE_HEADS * HEAD_SIZE), 2.0, 12.0, ((0, 32),)),
        "resp_len": jax.random.randint(part_keys[5], (1,), RESPONSE_ROWS // 4, RESPONSE_ROWS + 1).astype(jnp.int32),
        "residual": draw_residual(jax.random.fold_in(jax.random.fold_in(arg_keys[11], part), 71), part),
        "out_weight": noise(arg_keys[7], (QUERY_HEADS * HEAD_SIZE, D), (QUERY_HEADS * HEAD_SIZE) ** -0.5, 0.09375, ((1, 32),)),
        "norm_gain": draw_norm_gain(jax.random.fold_in(arg_keys[11], 71), part),
        "vocab_weight": noise(arg_keys[9], (D, VOCAB), (D // 9) ** -0.5, 0.25, ((1, 32),)),
        "targets": touch_ends(jax.random.randint(part_keys[10], (RESPONSE_ROWS,), 0, VOCAB), jax.random.fold_in(part_keys[10], 1), 0, VOCAB - 1).astype(jnp.int32),
    }


def reference(queries, prompt_keys, prompt_values, response_keys, response_values, resp_len, residual, out_weight, norm_gain, vocab_weight, targets):
    group_count = QUERY_HEADS // KEY_VALUE_HEADS
    length = resp_len[0]
    grouped_queries = queries.reshape(RESPONSE_ROWS, KEY_VALUE_HEADS, group_count, HEAD_SIZE).transpose(1, 0, 2, 3)
    heads_of_keys = jnp.concatenate([prompt_keys, response_keys], 0).reshape(PROMPT_TOKENS + RESPONSE_ROWS, KEY_VALUE_HEADS, HEAD_SIZE).transpose(1, 0, 2)
    heads_of_values = jnp.concatenate([prompt_values, response_values], 0).reshape(PROMPT_TOKENS + RESPONSE_ROWS, KEY_VALUE_HEADS, HEAD_SIZE).transpose(1, 0, 2)
    row_ids = jnp.arange(RESPONSE_ROWS, dtype=jnp.int32)
    resp_ok = (row_ids[None, :] <= row_ids[:, None]) & (row_ids[None, :] < length)
    allowed = jnp.concatenate([jnp.ones((RESPONSE_ROWS, PROMPT_TOKENS), dtype=bool), resp_ok], 1)

    def one_group(operands):
        query_block, key_block, value_block = operands
        scores = jnp.einsum('rgd,kd->rgk', query_block.astype(jnp.float32), key_block.astype(jnp.float32)) * HEAD_SIZE ** (-0.5)
        scores = jnp.where(allowed[:, None, :], scores, -jnp.inf)
        peak = lax.optimization_barrier(jnp.max(scores, -1, keepdims=True))
        weights = jnp.exp(scores - peak)
        total = lax.optimization_barrier(jnp.sum(weights, -1))
        output = jnp.einsum('rgk,kd->rgd', weights.astype(jnp.bfloat16).astype(jnp.float32), value_block.astype(jnp.float32))
        return output / total[..., None]
    outputs = lax.map(one_group, (grouped_queries, heads_of_keys, heads_of_values))
    attn = outputs.transpose(1, 0, 2, 3).reshape(RESPONSE_ROWS, QUERY_HEADS * HEAD_SIZE).astype(jnp.bfloat16)
    layer = residual.astype(jnp.float32) + jnp.dot(attn, out_weight, preferred_element_type=jnp.float32)
    layer_out = layer.astype(jnp.bfloat16)
    layer_float = layer_out.astype(jnp.float32)
    mean_square = lax.optimization_barrier(jnp.mean(layer_float * layer_float, -1, keepdims=True))
    normed = (layer_float * lax.rsqrt(mean_square + 1e-06) * norm_gain).astype(jnp.bfloat16)
    logits = jnp.dot(normed, vocab_weight, preferred_element_type=jnp.float32)
    top_logit = lax.optimization_barrier(jnp.max(logits, -1))
    log_total = top_logit + jnp.log(lax.optimization_barrier(jnp.sum(jnp.exp(logits - top_logit[:, None]), -1)))
    target_logit = jnp.take_along_axis(logits, targets[:, None].astype(jnp.int32), 1)[:, 0]
    row_loss = jnp.where(row_ids < length, log_total - target_logit, jnp.float32(0.0))
    return (layer_out, row_loss)
```

```python
import functools

import jax
import jax.numpy as jnp
from jax import lax
from jax.experimental import pallas as pl
from jax.experimental.pallas import tpu as pltpu
from jax.sharding import PartitionSpec as P

D = 4096
KEY_VALUE_HEADS = 4
HEAD_SIZE = 128
ROWS = 128
VOCAB_DEV = 2432
KEYS_DEV = 1024
LOG2E = 1.4426950408889634
SCORE_SCALE = LOG2E * HEAD_SIZE ** (-0.5)
MESH = pl.DeviceIdType.MESH
PLANE_ORDER = (0, 1, 3, 2)
PLANE_BACK = (0, 2, 1, 3)
F32 = jnp.float32
BF16 = jnp.bfloat16


def dot_nt(a, b):
    return lax.dot_general(a, b, (((1,), (1,)), ((), ())), preferred_element_type=F32)


def dot_nn(a, b):
    return jnp.dot(a, b, preferred_element_type=F32)


def eye_mask():
    return lax.broadcasted_iota(jnp.int32, (128, 128), 0) == lax.broadcasted_iota(
        jnp.int32, (128, 128), 1
    )


def to_row(column):
    return jnp.sum(jnp.where(eye_mask(), column, 0.0), axis=0, keepdims=True)


def to_column(row):
    return jnp.sum(jnp.where(eye_mask(), row, 0.0), axis=1, keepdims=True)


def drain(ref, sem):
    pltpu.make_async_copy(ref, ref, sem).wait()


def kernel(
    small, prompt_keys, prompt_values, length, residual, out_weight, gain, vocab_weight, targets,
    layer_out, row_loss,
    kbuf, vbuf, krb, vrb, qbuf, ostage, sstage, rbuf, rstat, mrg, abuf, wbuf, pown, ppart,
    gbuf, ssbuf, wv, acc, fbuf,
    local_sem, vocab_sem, kv_recv, w_recv, small_recv, q_recv, r_recv, own_sem, a_recv, p_recv,
    g_recv, h_recv, s_recv, f_recv, send_sem,
):
    me = lax.axis_index("seq")
    z, x, c = me // 8, (me // 2) % 4, me % 2
    chip = me // 2
    other = 1 - c
    sibling = chip * 2 + other

    def rel_chip(dz, dx):
        return lax.rem(z + dz, 4) * 4 + lax.rem(x + dx, 4)

    def send(src, dst, sem, target, kind):
        pltpu.make_async_remote_copy(
            src_ref=src, dst_ref=dst, send_sem=send_sem.at[kind], recv_sem=sem,
            device_id={"seq": target}, device_id_type=MESH,
        ).start()

    my_cols = pl.ds(pl.multiple_of(c * 256, 256), 256)
    other_cols = pl.ds(pl.multiple_of(other * 256, 256), 256)
    my_half = pl.ds(pl.multiple_of(c * 2048, 2048), 2048)
    other_half = pl.ds(pl.multiple_of(other * 2048, 2048), 2048)
    w_lane = pl.ds(pl.multiple_of(c * 128, 128), 128)

    barrier = pltpu.get_barrier_semaphore()

    def greet(i, carry):
        pl.semaphore_signal(
            barrier, inc=1, device_id={"seq": lax.rem(me + i, 32)}, device_id_type=MESH
        )
        return carry

    lax.fori_loop(1, 32, greet, 0)

    own_copies = [
        pltpu.make_async_copy(prompt_keys.at[:, my_cols], kbuf.at[c], local_sem.at[0]),
        pltpu.make_async_copy(prompt_values.at[:, my_cols], vbuf.at[c], local_sem.at[1]),
        pltpu.make_async_copy(out_weight.at[my_half, :], wbuf.at[:, w_lane], local_sem.at[2]),
    ]
    for copy in own_copies:
        copy.start()
    vocab_copies = [
        pltpu.make_async_copy(
            vocab_weight.at[pl.ds(i * 1024, 1024), :], wv.at[pl.ds(i * 1024, 1024), :],
            vocab_sem.at[i],
        )
        for i in range(4)
    ]

    krb[:, 32:, :] = jnp.zeros((2, 96, 128), BF16)
    vrb[:, 32:, :] = jnp.zeros((2, 96, 128), BF16)
    for j in range(2):
        krb[j, pl.ds(pl.multiple_of(c * 16, 16), 16), :] = small[2 * c + j, 32:48, :]
        vrb[j, pl.ds(pl.multiple_of(c * 16, 16), 16), :] = small[2 * c + j, 48:64, :]
        qbuf[z, j, pl.ds(pl.multiple_of((x * 2 + c) * 32, 32), 32), :] = small[2 * c + j, 0:32, :]

    pl.semaphore_wait(barrier, 31)

    resp_rows = pl.ds(pl.multiple_of(c * 16, 16), 16)
    q_rows = pl.ds(pl.multiple_of((x * 2 + c) * 32, 32), 32)

    def send_plane(u):
        tz = lax.rem(z + PLANE_ORDER[u], 4)

        def one(i, carry):
            tx = lax.rem(x + i // 2, 4)
            tc = lax.rem(c + i, 2)
            target = (tz * 4 + tx) * 2 + tc
            for j in range(2):
                send(
                    small.at[2 * tc + j, pl.ds(0, 32), :], qbuf.at[z, j, q_rows, :],
                    q_recv.at[PLANE_BACK[u]], target, 0,
                )
            return carry

        lax.fori_loop(1 if u == 0 else 0, 8, one, 0)

    send_plane(0)
    for j in range(2):
        send(small.at[2 * other + j, pl.ds(32, 16), :], krb.at[j, resp_rows, :], small_recv.at[0], sibling, 1)
        send(small.at[2 * other + j, pl.ds(48, 16), :], vrb.at[j, resp_rows, :], small_recv.at[0], sibling, 1)
    send(prompt_keys.at[:, other_cols], kbuf.at[c], kv_recv.at[0], sibling, 2)
    send(prompt_values.at[:, other_cols], vbuf.at[c], kv_recv.at[1], sibling, 2)
    send_plane(2)
    send_plane(1)
    send_plane(3)
    send(out_weight.at[other_half, :], wbuf.at[:, w_lane], w_recv.at[0], sibling, 3)
    for copy in vocab_copies:
        copy.start()

    live = length[0]
    key_column = lax.broadcasted_iota(jnp.int32, (256, 128), 1)
    key_id = chip * 8 + (key_column // 16) * 4 + key_column % 16
    key_ok = (key_column < 32) & (key_column % 16 < 4) & (key_id < live)
    row_in_plane = lax.broadcasted_iota(jnp.int32, (256, 128), 0) // 8

    for u in range(4):
        t = lax.rem(z + PLANE_ORDER[u], 4)
        drain(qbuf.at[0, :, pl.ds(0, 224 if u == 0 else 256), :], q_recv.at[u])
        if u == 0:
            drain(krb.at[:, pl.ds(0, 32), :], small_recv.at[0])
            own_copies[0].wait()
            drain(kbuf.at[0], kv_recv.at[0])
        visible = key_ok & (key_id <= t * 32 + row_in_plane)
        for j in range(2):
            cols = slice(j * 128, (j + 1) * 128)
            q = qbuf[t, j]
            s0 = dot_nt(q, kbuf[0, :, cols])
            s1 = dot_nt(q, kbuf[1, :, cols])
            sr = jnp.where(visible, dot_nt(q, krb[j]), -jnp.inf)
            peak = jnp.maximum(
                jnp.maximum(jnp.max(s0, 1, keepdims=True), jnp.max(s1, 1, keepdims=True)),
                jnp.max(sr, 1, keepdims=True),
            ) * SCORE_SCALE
            p0 = jnp.exp2(s0 * SCORE_SCALE - peak)
            p1 = jnp.exp2(s1 * SCORE_SCALE - peak)
            pr = jnp.exp2(sr * SCORE_SCALE - peak)
            total = (
                jnp.sum(p0, 1, keepdims=True) + jnp.sum(p1, 1, keepdims=True)
                + jnp.sum(pr, 1, keepdims=True)
            )
            if u == 0 and j == 0:
                own_copies[1].wait()
                drain(vbuf.at[0], kv_recv.at[1])
            o = (
                dot_nn(p0.astype(BF16), vbuf[0, :, cols])
                + dot_nn(p1.astype(BF16), vbuf[1, :, cols])
                + dot_nn(pr.astype(BF16), vrb[j])
            )
            ostage[u, j] = o.astype(BF16)
            for half in range(2):
                rows = slice(half * 128, (half + 1) * 128)
                sstage[u, j, half, 0:1, :] = to_row(peak[rows])
                sstage[u, j, half, 1:2, :] = to_row(total[rows])
                owner = (t * 4 + 2 * half + j) * 2 + c
                part = ostage.at[u, j, pl.ds(half * 128, 128), :]
                stat = sstage.at[u, j, half]

                def to_other():
                    send(part, rbuf.at[chip], r_recv.at[0], owner, 4)
                    send(stat, rstat.at[chip], r_recv.at[1], owner, 5)

                def to_self():
                    pltpu.make_async_copy(part, rbuf.at[chip], own_sem.at[0]).start()
                    pltpu.make_async_copy(stat, rstat.at[chip], own_sem.at[1]).start()

                if u == 0:
                    pl.when(owner != me)(to_other)
                    pl.when(owner == me)(to_self)
                else:
                    to_other()

    drain(rstat.at[pl.ds(0, 15)], r_recv.at[1])
    drain(rstat.at[0], own_sem.at[1])
    peaks = rstat[:, 0, :]
    weight = jnp.exp2(peaks - jnp.max(peaks, 0, keepdims=True))
    weight = weight / jnp.sum(weight * rstat[:, 1, :], 0, keepdims=True)
    weight = jnp.concatenate([weight, jnp.zeros((112, 128), F32)], 0).T
    drain(rbuf.at[pl.ds(0, 15)], r_recv.at[0])
    drain(rbuf.at[0], own_sem.at[0])
    merged = weight[:, 0:1] * rbuf[0].astype(F32)
    for k in range(1, 16):
        merged += weight[:, k : k + 1] * rbuf[k].astype(F32)
    mrg[...] = merged
    block = jnp.concatenate([mrg[pl.ds(h, 16, stride=8), :] for h in range(8)], 1)
    head_group, row_group = lax.rem(x, 2), z * 2 + x // 2
    abuf[head_group, row_group] = block.astype(BF16)

    def spread_attn(i, carry):
        target = rel_chip(i // 4, i % 4) * 2 + c
        mine = abuf.at[head_group, row_group]
        send(mine, mine, a_recv.at[0], target, 6)
        return carry

    lax.fori_loop(1, 16, spread_attn, 0)
    own_copies[2].wait()
    drain(wbuf.at[:, pl.ds(0, 128)], w_recv.at[0])
    drain(rbuf.at[pl.ds(0, 15)], a_recv.at[0])
    projected = dot_nn(abuf[0].reshape(128, 1024), wbuf[pl.ds(0, 1024), :]) + dot_nn(
        abuf[1].reshape(128, 1024), wbuf[pl.ds(1024, 1024), :]
    )
    pown[0] = projected[:, :128]
    pown[1] = projected[:, 128:]
    send(pown.at[other], ppart, p_recv.at[0], sibling, 7)
    base = residual[...].astype(F32) + pown[c]
    drain(ppart, p_recv.at[0])
    layer = (base + ppart[...]).astype(BF16)
    layer_out[...] = layer
    layer = layer.astype(F32)
    gbuf[chip, c] = (layer * gain[...]).astype(BF16)
    ssbuf[me] = to_row(jnp.sum(layer * layer, 1, keepdims=True))

    def spread_features(i, carry):
        target = rel_chip(i // 4, i % 4) * 2 + c
        mine = gbuf.at[chip, c]
        send(mine, mine, g_recv.at[i], target, 8)
        return carry

    lax.fori_loop(1, 16, spread_features, 0)
    send(gbuf.at[chip, c], gbuf.at[chip, c], h_recv.at[0], sibling, 9)

    def spread_squares(i, carry):
        mine = ssbuf.at[me]
        send(mine, mine, s_recv.at[0], lax.rem(me + i, 32), 10)
        return carry

    lax.fori_loop(1, 32, spread_squares, 0)

    for copy in vocab_copies:
        copy.wait()
    acc[...] = jnp.zeros_like(acc)

    def logits_of(i):
        source = lax.rem(z + 4 - i // 4, 4) * 4 + lax.rem(x + 4 - i % 4, 4)
        return source

    def step(i, carry):
        source = logits_of(i)

        @pl.when(i < 16)
        def _():
            @pl.when(i > 0)
            def _():
                drain(gbuf.at[0, 0], g_recv.at[i])
                block = gbuf.at[source, c]
                send(block, block, h_recv.at[i], sibling, 9)

        @pl.when(i > 0)
        def _():
            prev = logits_of(i - 1)
            drain(gbuf.at[0, 0], h_recv.at[i - 1])
            features = jnp.concatenate([gbuf[prev, 0], gbuf[prev, 1]], 1)
            acc[...] += dot_nn(features, wv[pl.ds(pl.multiple_of(prev * 256, 256), 256), :])

        return carry

    lax.fori_loop(0, 17, step, 0)

    drain(ssbuf.at[pl.ds(0, 31)], s_recv.at[0])
    squares = jnp.sum(ssbuf[:, 0, :], 0, keepdims=True)
    inverse = to_column(lax.rsqrt(squares / D + 1e-06))
    logits = acc[...] * inverse
    top = jnp.max(logits, 1, keepdims=True)
    exp_total = jnp.sum(jnp.exp(logits - top), 1, keepdims=True)
    target = to_column(targets[...].astype(F32)).astype(jnp.int32) - me * VOCAB_DEV
    hit = lax.broadcasted_iota(jnp.int32, (ROWS, VOCAB_DEV), 1) == target
    target_logit = jnp.sum(jnp.where(hit, logits, 0.0), 1, keepdims=True)
    fbuf[me, 0:1, :] = to_row(top)
    fbuf[me, 1:2, :] = to_row(exp_total)
    fbuf[me, 2:3, :] = to_row(target_logit)

    def spread_totals(i, carry):
        mine = fbuf.at[me]
        send(mine, mine, f_recv.at[0], lax.rem(me + i, 32), 11)
        return carry

    lax.fori_loop(1, 32, spread_totals, 0)
    drain(fbuf.at[pl.ds(0, 31)], f_recv.at[0])
    tops = fbuf[:, 0, :]
    top = jnp.max(tops, 0, keepdims=True)
    whole = jnp.sum(fbuf[:, 1, :] * jnp.exp(tops - top), 0, keepdims=True)
    loss = top + jnp.log(whole) - jnp.sum(fbuf[:, 2, :], 0, keepdims=True)
    row_ids = lax.broadcasted_iota(jnp.int32, (1, ROWS), 1)
    row_loss[...] = jnp.where(row_ids < live, loss, 0.0)

    drain(kbuf.at[0, pl.ds(0, 992), :], send_sem.at[0])
    drain(krb.at[:, pl.ds(0, 32), :], send_sem.at[1])
    drain(kbuf, send_sem.at[2])
    drain(wbuf.at[:, pl.ds(0, 128)], send_sem.at[3])
    owns = 1
    drain(rbuf.at[pl.ds(0, 16 - owns)], send_sem.at[4])
    drain(rstat.at[pl.ds(0, 16 - owns)], send_sem.at[5])
    drain(rbuf.at[pl.ds(0, 15)], send_sem.at[6])
    drain(ppart, send_sem.at[7])
    drain(rbuf.at[pl.ds(0, 15)], send_sem.at[8])
    drain(rbuf, send_sem.at[9])
    drain(ssbuf.at[pl.ds(0, 31)], send_sem.at[10])
    drain(fbuf.at[pl.ds(0, 31)], send_sem.at[11])


def local(
    queries, prompt_keys, prompt_values, response_keys, response_values, resp_len, residual,
    out_weight, norm_gain, vocab_weight, targets,
):
    rows = queries.shape[0]

    def by_key_head(a):
        return a.reshape(rows, KEY_VALUE_HEADS, -1, HEAD_SIZE).transpose(1, 0, 2, 3).reshape(
            KEY_VALUE_HEADS, -1, HEAD_SIZE
        )

    pad = ((0, 0), (0, 16 - rows), (0, 0))
    small = jnp.concatenate(
        [
            by_key_head(queries),
            jnp.pad(by_key_head(response_keys), pad),
            jnp.pad(by_key_head(response_values), pad),
        ],
        1,
    )
    vmem = pl.BlockSpec(memory_space=pltpu.VMEM)
    hbm = pl.BlockSpec(memory_space=pl.ANY)
    dma = pltpu.SemaphoreType.DMA
    layer_out, row_loss = pl.pallas_call(
        kernel,
        out_shape=(
            jax.ShapeDtypeStruct((ROWS, 128), BF16),
            jax.ShapeDtypeStruct((1, ROWS), F32),
        ),
        in_specs=[vmem, hbm, hbm, pl.BlockSpec(memory_space=pltpu.SMEM), vmem, hbm, vmem, hbm, vmem],
        out_specs=(vmem, vmem),
        scratch_shapes=[
            pltpu.VMEM((2, KEYS_DEV, 256), BF16),
            pltpu.VMEM((2, KEYS_DEV, 256), BF16),
            pltpu.VMEM((2, 128, 128), BF16),
            pltpu.VMEM((2, 128, 128), BF16),
            pltpu.VMEM((4, 2, 256, 128), BF16),
            pltpu.VMEM((4, 2, 256, 128), BF16),
            pltpu.VMEM((4, 2, 2, 8, 128), F32),
            pltpu.VMEM((16, 128, 128), BF16),
            pltpu.VMEM((16, 8, 128), F32),
            pltpu.VMEM((128, 128), F32),
            pltpu.VMEM((2, 8, 16, 1024), BF16),
            pltpu.VMEM((2048, 256), BF16),
            pltpu.VMEM((2, 128, 128), F32),
            pltpu.VMEM((128, 128), F32),
            pltpu.VMEM((16, 2, 128, 128), BF16),
            pltpu.VMEM((32, 1, 128), F32),
            pltpu.VMEM((D, VOCAB_DEV), BF16),
            pltpu.VMEM((ROWS, VOCAB_DEV), F32),
            pltpu.VMEM((32, 8, 128), F32),
            dma((3,)),
            dma((4,)),
            dma((2,)),
            dma((1,)),
            dma((1,)),
            dma((4,)),
            dma((2,)),
            dma((2,)),
            dma((1,)),
            dma((1,)),
            dma((16,)),
            dma((16,)),
            dma((1,)),
            dma((1,)),
            dma((12,)),
        ],
        compiler_params=pltpu.CompilerParams(
            collective_id=0, has_side_effects=True, vmem_limit_bytes=56 * 1024 * 1024
        ),
        name="score_response",
    )(
        small, prompt_keys, prompt_values, resp_len, residual, out_weight,
        norm_gain.reshape(1, 128), vocab_weight, targets.reshape(1, ROWS),
    )
    return layer_out, row_loss.reshape(ROWS)


def solution(mesh):
    placed = (
        P(("batch", "seq"), None),
        P(("batch", "seq"), None),
        P(("batch", "seq"), None),
        P(("batch", "seq"), None),
        P(("batch", "seq"), None),
        P("batch"),
        P("batch", "seq"),
        P(None, "seq"),
        P("seq"),
        P(None, "seq"),
        P("batch"),
    )
    return jax.shard_map(
        local,
        mesh=mesh,
        in_specs=placed,
        out_specs=(P("batch", "seq"), P("batch")),
        check_vma=False,
    )
```

```python
import functools

import jax
import jax.numpy as jnp
from jax import lax
from jax.experimental import pallas as pl
from jax.experimental.pallas import tpu as pltpu
from jax.sharding import PartitionSpec as P

D = 4096
KEY_VALUE_HEADS = 4
HEAD_SIZE = 128
ROWS = 128
VOCAB_DEV = 2432
KEYS_DEV = 1024
LOG2E = 1.4426950408889634
SCORE_SCALE = LOG2E * HEAD_SIZE ** (-0.5)
MESH = pl.DeviceIdType.MESH
F32 = jnp.float32
BF16 = jnp.bfloat16


def dot_nt(a, b):
    return lax.dot_general(a, b, (((1,), (1,)), ((), ())), preferred_element_type=F32)


def dot_nn(a, b):
    return jnp.dot(a, b, preferred_element_type=F32)


def eye_mask():
    return lax.broadcasted_iota(jnp.int32, (128, 128), 0) == lax.broadcasted_iota(
        jnp.int32, (128, 128), 1
    )


def to_row(column):
    return jnp.sum(jnp.where(eye_mask(), column, 0.0), axis=0, keepdims=True)


def to_column(row):
    return jnp.sum(jnp.where(eye_mask(), row, 0.0), axis=1, keepdims=True)


def drain(ref, sem):
    pltpu.make_async_copy(ref, ref, sem).wait()


def kernel(
    queries, response_keys, response_values, prompt_keys, prompt_values, length, residual_in,
    out_weight, gain_in, vocab_weight, targets_in,
    layer_out, row_loss,
    residual, gain, targets, spread, small, resp, respbuf, kbuf, vbuf, qbuf, ostage, sstage, rbuf, rstat, mrg, abuf, wbuf,
    pown, ppart, gbuf, ssbuf, ssplane, wv, acc, fbuf,
    local_sem, vocab_sem, kv_recv, w_recv, small_recv, q_ring, q_diag, r_recv, own_sem, a_recv,
    p_recv, g_ring, g_diag, h_recv, s_recv, f_recv, send_sem,
):
    me = lax.axis_index("seq")
    z, x, c = me // 8, (me // 2) % 4, me % 2
    chip = me // 2
    other = 1 - c
    sibling = chip * 2 + other

    def turn(a, d):
        return lax.rem(a + d, 4)

    def device(cz, cx, core):
        return (cz * 4 + cx) * 2 + core

    def send(src, dst, sem, target, kind):
        pltpu.make_async_remote_copy(
            src_ref=src, dst_ref=dst, send_sem=send_sem.at[kind], recv_sem=sem,
            device_id={"seq": target}, device_id_type=MESH,
        ).start()

    my_cols = pl.ds(pl.multiple_of(c * 256, 256), 256)
    other_cols = pl.ds(pl.multiple_of(other * 256, 256), 256)
    my_half = pl.ds(pl.multiple_of(c * 2048, 2048), 2048)
    other_half = pl.ds(pl.multiple_of(other * 2048, 2048), 2048)
    w_lane = pl.ds(pl.multiple_of(c * 128, 128), 128)

    barrier = pltpu.get_barrier_semaphore()
    x_peers = [device(z, turn(x, d), core) for d in (2, 1, 3) for core in (c, other)]
    z_peers = [device(turn(z, d), x, core) for d in (2, 1, 3) for core in (c, other)]
    for peer in z_peers + x_peers + [sibling]:
        pl.semaphore_signal(barrier, inc=1, device_id={"seq": peer}, device_id_type=MESH)

    own_copies = [
        pltpu.make_async_copy(prompt_keys.at[:, my_cols], kbuf.at[c], local_sem.at[0]),
        pltpu.make_async_copy(prompt_values.at[:, my_cols], vbuf.at[c], local_sem.at[1]),
        pltpu.make_async_copy(out_weight.at[my_half, :], wbuf.at[:, w_lane], local_sem.at[2]),
        pltpu.make_async_copy(residual_in, residual, local_sem.at[3]),
        pltpu.make_async_copy(gain_in, gain, local_sem.at[4]),
        pltpu.make_async_copy(targets_in, targets, local_sem.at[5]),
    ]
    for copy in own_copies:
        copy.start()
    vocab_copies = [
        pltpu.make_async_copy(
            vocab_weight.at[pl.ds(i * 1024, 1024), :], wv.at[pl.ds(i * 1024, 1024), :],
            vocab_sem.at[i],
        )
        for i in range(4)
    ]

    wide = queries[...].astype(F32)
    for head in range(32):
        spread[head // 8, pl.ds(head % 8, 4, stride=8), :] = wide[:, head * 128 : head * 128 + 128]
    nothing = jnp.zeros((12, 128), F32)
    for g in range(4):
        cols = slice(g * 128, g * 128 + 128)
        small[g] = spread[g].astype(BF16)
        resp[g, 0:16, :] = jnp.concatenate([response_keys[:, cols].astype(F32), nothing], 0).astype(BF16)
        resp[g, 16:32, :] = jnp.concatenate([response_values[:, cols].astype(F32), nothing], 0).astype(BF16)
    q_rows = pl.ds(pl.multiple_of((x * 2 + c) * 32, 32), 32)
    my_heads, other_heads = pl.ds(2 * c, 2), pl.ds(2 * other, 2)
    for j in range(2):
        qbuf[z, j, q_rows, :] = small[2 * c + j]
        respbuf[c, j] = resp[2 * c + j]

    pl.semaphore_wait(barrier, 13)

    send(resp.at[other_heads], respbuf.at[c], small_recv.at[0], sibling, 1)
    def q_half(cz, cx, part):
        return qbuf.at[cz, part, pl.ds(pl.multiple_of(cx * 64, 64), 64), :]

    mine = qbuf.at[z, :, q_rows, :]
    send(small.at[other_heads], mine, q_ring.at[0, 0], sibling, 0)
    for d in (1, 3, 2):
        for core in (c, other):
            heads = small.at[pl.ds(2 * core, 2)]
            send(heads, mine, q_ring.at[0, 4 - d], device(z, turn(x, d), core), 0)
            send(heads, mine, q_ring.at[1, 4 - d], device(turn(z, d), x, core), 0)
    send(prompt_keys.at[:, other_cols], kbuf.at[c], kv_recv.at[0], sibling, 2)
    send(prompt_values.at[:, other_cols], vbuf.at[c], kv_recv.at[1], sibling, 2)
    for d in (1, 3, 2):
        sx, sz = turn(x, d), turn(z, d)
        drain(qbuf.at[0, 0, pl.ds(0, 128), :], q_ring.at[0, d])
        for e in (1, 3, 2):
            block = q_half(z, sx, 0)
            send(block, block, q_diag.at[0, (4 - e) * 4 + d], device(turn(z, e), x, c), 12)
        drain(qbuf.at[0, 0, pl.ds(0, 128), :], q_ring.at[1, d])
        for e in (1, 3, 2):
            block = q_half(sz, x, 1)
            send(block, block, q_diag.at[1, d * 4 + 4 - e], device(z, turn(x, e), c), 12)
    drain(qbuf.at[0, 0, pl.ds(0, 64), :], q_ring.at[0, 0])
    send(out_weight.at[other_half, :], wbuf.at[:, w_lane], w_recv.at[0], sibling, 3)
    for copy in vocab_copies:
        copy.start()

    live = length[0]
    key_column = lax.broadcasted_iota(jnp.int32, (256, 32), 1)
    key_id = chip * 8 + (key_column // 16) * 4 + key_column % 16
    key_ok = (key_column % 16 < 4) & (key_id < live)
    row_in_plane = lax.broadcasted_iota(jnp.int32, (256, 32), 0) // 8
    drain(resp.at[pl.ds(0, 2)], small_recv.at[0])
    own_copies[0].wait()
    drain(kbuf.at[0], kv_recv.at[0])
    own_copies[1].wait()
    drain(vbuf.at[0], kv_recv.at[1])

    def with_ones(v):
        return jnp.concatenate([v, jnp.ones_like(v)], 1)

    for u, offset in enumerate((0, 1 + 2 * (x % 2), 2, 3 - 2 * (x % 2))):
        t = turn(z, offset)
        if u > 0:
            for dx in (1, 3, 2):
                for part in range(2):
                    drain(qbuf.at[0, 0, pl.ds(0, 64), :], q_diag.at[part, offset * 4 + dx])

        visible = key_ok & (key_id <= t * 32 + row_in_plane)
        for j in range(2):
            cols = slice(j * 128, (j + 1) * 128)
            q = qbuf[t, j]
            s0 = dot_nt(q, kbuf[0, :, cols])
            s1 = dot_nt(q, kbuf[1, :, cols])
            resp_keys = jnp.concatenate([respbuf[0, j, 0:16, :], respbuf[1, j, 0:16, :]], 0)
            resp_values = jnp.concatenate([respbuf[0, j, 16:32, :], respbuf[1, j, 16:32, :]], 0)
            sr = jnp.where(visible, dot_nt(q, resp_keys), -jnp.inf)
            peak = jnp.maximum(
                jnp.maximum(jnp.max(s0, 1, keepdims=True), jnp.max(s1, 1, keepdims=True)),
                jnp.max(sr, 1, keepdims=True),
            ) * SCORE_SCALE
            p0 = jnp.exp2(s0 * SCORE_SCALE - peak)
            p1 = jnp.exp2(s1 * SCORE_SCALE - peak)
            pr = jnp.exp2(sr * SCORE_SCALE - peak)
            o = (
                dot_nn(p0.astype(BF16), with_ones(vbuf[0, :, cols]))
                + dot_nn(p1.astype(BF16), with_ones(vbuf[1, :, cols]))
                + dot_nn(pr.astype(BF16), with_ones(resp_values))
            )
            total = o[:, 128:]
            ostage[u, j] = o[:, :128].astype(BF16)
            for half in range(2):
                rows = slice(half * 128, (half + 1) * 128)
                sstage[u, j, half, 0:1, :] = to_row(peak[rows])
                sstage[u, j, half, 1:2, :] = to_row(total[rows])
                quarter = 2 * half + j
                owner = device(t, quarter, c)
                part = ostage.at[u, j, pl.ds(half * 128, 128), :]
                stat = sstage.at[u, j, half]

                def to_owner():
                    send(part, rbuf.at[chip], r_recv.at[0], owner, 4)
                    send(stat, rstat.at[chip], r_recv.at[1], owner, 5)

                if u > 0:
                    to_owner()
                    continue
                pl.when(owner != me)(to_owner)

                @pl.when(owner == me)
                def _():
                    pltpu.make_async_copy(part, rbuf.at[chip], own_sem.at[0]).start()
                    pltpu.make_async_copy(stat, rstat.at[chip], own_sem.at[1]).start()

    drain(rstat.at[pl.ds(0, 15)], r_recv.at[1])
    drain(rstat.at[0], own_sem.at[1])
    peaks = rstat[:, 0, :]
    weight = jnp.exp2(peaks - jnp.max(peaks, 0, keepdims=True))
    weight = weight / jnp.sum(weight * rstat[:, 1, :], 0, keepdims=True)
    weight = jnp.concatenate([weight, jnp.zeros((112, 128), F32)], 0).T
    drain(rbuf.at[pl.ds(0, 15)], r_recv.at[0])
    drain(rbuf.at[0], own_sem.at[0])
    merged = weight[:, 0:1] * rbuf[0].astype(F32)
    for k in range(1, 16):
        merged += weight[:, k : k + 1] * rbuf[k].astype(F32)
    mrg[...] = merged
    block = jnp.concatenate([mrg[pl.ds(h, 16, stride=8), :] for h in range(8)], 1)
    abuf[z, x] = block.astype(BF16)

    def torus_distance(d):
        return min(d[0], 4 - d[0]) + min(d[1], 4 - d[1])

    far_first = sorted([(dz, dx) for dz in range(4) for dx in range(4)], key=lambda d: -torus_distance(d))
    for dz, dx in far_first[:-1]:
        send(abuf.at[z, x], abuf.at[z, x], a_recv.at[0], device(turn(z, dz), turn(x, dx), c), 6)
    for copy in own_copies[2:]:
        copy.wait()
    drain(wbuf.at[:, pl.ds(0, 128)], w_recv.at[0])
    drain(rbuf.at[pl.ds(0, 15)], a_recv.at[0])
    projected = None
    for j in range(2):
        attn = jnp.concatenate(
            [abuf[t, 2 * half + j] for t in range(4) for half in range(2)], 0
        )
        term = dot_nn(attn, wbuf[pl.ds(j * 1024, 1024), :])
        projected = term if j == 0 else projected + term
    pown[0] = projected[:, :128]
    pown[1] = projected[:, 128:]
    send(pown.at[other], ppart, p_recv.at[0], sibling, 7)
    base = residual[...].astype(F32) + pown[c]
    drain(ppart, p_recv.at[0])
    layer = (base + ppart[...]).astype(BF16)
    layer_out[...] = layer
    layer = layer.astype(F32)
    gbuf[z, x, c] = (layer * gain[...]).astype(BF16)
    ssbuf[x * 2 + c] = to_row(jnp.sum(layer * layer, 1, keepdims=True))

    def gather(full, half, ring, diag, kind, on_ring):
        for d in (1, 3, 2):
            send(full(z, x), full(z, x), ring.at[0, 4 - d], device(z, turn(x, d), c), kind)
            send(full(z, x), full(z, x), ring.at[1, 4 - d], device(turn(z, d), x, c), kind)
        for d in (1, 3, 2):
            sx, sz = turn(x, d), turn(z, d)
            drain(full(0, 0), ring.at[0, d])
            for e in (1, 3, 2):
                block = half(z, sx, 0)
                send(block, block, diag.at[0, (4 - e) * 4 + d], device(turn(z, e), x, c), kind)
            on_ring(z, sx, d)
            drain(full(0, 0), ring.at[1, d])
            for e in (1, 3, 2):
                block = half(sz, x, 1)
                send(block, block, diag.at[1, d * 4 + 4 - e], device(z, turn(x, e), c), kind)
            on_ring(sz, x, d * 4)

    def g_full(cz, cx):
        return gbuf.at[cz, cx, c]

    def g_half(cz, cx, part):
        return gbuf.at[cz, cx, c, pl.ds(part * 64, 64), :]

    def to_sibling(cz, cx, index):
        send(g_full(cz, cx), g_full(cz, cx), h_recv.at[index], sibling, 9)

    to_sibling(z, x, 0)
    for peer in x_peers + [sibling]:
        mine = ssbuf.at[x * 2 + c]
        send(mine, mine, s_recv.at[0], peer, 10)
    gather(g_full, g_half, g_ring, g_diag, 8, to_sibling)
    drain(ssbuf.at[pl.ds(0, 7)], s_recv.at[0])
    ssplane[z] = jnp.sum(ssbuf[:, 0, :], 0, keepdims=True)
    for d in (2, 1, 3):
        send(ssplane.at[z], ssplane.at[z], s_recv.at[1], device(turn(z, d), x, c), 11)

    def plane_features(cz):
        return jnp.concatenate([gbuf[cz, cx, core] for cx in range(4) for core in range(2)], 1)

    def plane_rows(cz):
        return pl.ds(pl.multiple_of(cz * 1024, 1024), 1024)

    for copy in vocab_copies:
        copy.wait()
    for dx in range(4):
        drain(gbuf.at[0, 0, 0], h_recv.at[dx])
    acc[...] = dot_nn(plane_features(z), wv[plane_rows(z), :])
    for dz in (1, 3, 2):
        for dx in (1, 3, 2):
            for part in range(2):
                drain(g_half(0, 0, part), g_diag.at[part, dz * 4 + dx])
            to_sibling(turn(z, dz), turn(x, dx), dz * 4 + dx)
    for dz in (1, 3, 2):
        for dx in range(4):
            drain(gbuf.at[0, 0, 0], h_recv.at[dz * 4 + dx])
    planes = [turn(z, dz) for dz in (1, 2, 3)]
    features = [plane_features(cz) for cz in planes]
    for n in range(0, VOCAB_DEV, 512):
        cols = slice(n, min(n + 512, VOCAB_DEV))
        part = acc[:, cols]
        for cz, f in zip(planes, features):
            part += dot_nn(f, wv[plane_rows(cz), cols])
        acc[:, cols] = part

    drain(ssplane.at[pl.ds(0, 3)], s_recv.at[1])
    squares = jnp.sum(ssplane[:, 0, :], 0, keepdims=True)
    inverse = to_column(lax.rsqrt(squares / D + 1e-06))
    logits = acc[...] * inverse
    top = jnp.max(logits, 1, keepdims=True)
    exp_total = jnp.sum(jnp.exp(logits - top), 1, keepdims=True)
    target = to_column(targets[...].astype(F32)).astype(jnp.int32) - me * VOCAB_DEV
    hit = lax.broadcasted_iota(jnp.int32, (ROWS, VOCAB_DEV), 1) == target
    target_logit = jnp.sum(jnp.where(hit, logits, 0.0), 1, keepdims=True)
    fbuf[me] = jnp.concatenate([to_row(top), to_row(exp_total), to_row(target_logit)], 1)

    for dz, dx in far_first:
        for core in (c, other):
            if (dz, dx) != (0, 0) or core is other:
                target_device = device(turn(z, dz), turn(x, dx), core)
                send(fbuf.at[me], fbuf.at[me], f_recv.at[0], target_device, 13)
    drain(fbuf.at[pl.ds(0, 31)], f_recv.at[0])
    tops = fbuf[:, 0, 0:128]
    top = jnp.max(tops, 0, keepdims=True)
    whole = jnp.sum(fbuf[:, 0, 128:256] * jnp.exp(tops - top), 0, keepdims=True)
    loss = top + jnp.log(whole) - jnp.sum(fbuf[:, 0, 256:384], 0, keepdims=True)
    row_ids = lax.broadcasted_iota(jnp.int32, (1, ROWS), 1)
    row_loss[...] = jnp.where(row_ids < live, loss, 0.0)

    drain(kbuf.at[0, pl.ds(0, 416), :], send_sem.at[0])
    drain(resp.at[pl.ds(0, 2)], send_sem.at[1])
    drain(kbuf, send_sem.at[2])
    drain(wbuf.at[:, pl.ds(0, 128)], send_sem.at[3])
    drain(rbuf.at[pl.ds(0, 15)], send_sem.at[4])
    drain(rstat.at[pl.ds(0, 15)], send_sem.at[5])
    drain(rbuf.at[pl.ds(0, 15)], send_sem.at[6])
    drain(ppart, send_sem.at[7])
    drain(rbuf.at[pl.ds(0, 15)], send_sem.at[8])
    drain(rbuf, send_sem.at[9])
    drain(ssbuf.at[pl.ds(0, 7)], send_sem.at[10])
    drain(ssplane.at[pl.ds(0, 3)], send_sem.at[11])
    drain(kbuf.at[0, pl.ds(0, 576), :], send_sem.at[12])
    drain(fbuf.at[pl.ds(0, 31)], send_sem.at[13])


def hand_over(layer, loss, layer_out, loss_out):
    layer_out[...] = layer[...]
    loss_out[...] = loss[...]


def local(
    queries, prompt_keys, prompt_values, response_keys, response_values, resp_len, residual,
    out_weight, norm_gain, vocab_weight, targets,
):
    vmem = pl.BlockSpec(memory_space=pltpu.VMEM)
    hbm = pl.BlockSpec(memory_space=pl.ANY)
    dma = pltpu.SemaphoreType.DMA
    shapes = (
        jax.ShapeDtypeStruct((ROWS, 128), BF16),
        jax.ShapeDtypeStruct((1, ROWS), F32),
    )
    results = pl.pallas_call(
        kernel,
        out_shape=shapes,
        in_specs=[
            vmem, vmem, vmem, hbm, hbm, pl.BlockSpec(memory_space=pltpu.SMEM), hbm, hbm, hbm,
            hbm, hbm,
        ],
        out_specs=(vmem, vmem),
        scratch_shapes=[
            pltpu.VMEM((ROWS, 128), BF16),
            pltpu.VMEM((1, 128), F32),
            pltpu.VMEM((1, ROWS), jnp.int32),
            pltpu.VMEM((4, 32, 128), F32),
            pltpu.VMEM((4, 32, 128), BF16),
            pltpu.VMEM((4, 32, 128), BF16),
            pltpu.VMEM((2, 2, 32, 128), BF16),
            pltpu.VMEM((2, KEYS_DEV, 256), BF16),
            pltpu.VMEM((2, KEYS_DEV, 256), BF16),
            pltpu.VMEM((4, 2, 256, 128), BF16),
            pltpu.VMEM((4, 2, 256, 128), BF16),
            pltpu.VMEM((4, 2, 2, 8, 128), F32),
            pltpu.VMEM((16, 128, 128), BF16),
            pltpu.VMEM((16, 8, 128), F32),
            pltpu.VMEM((128, 128), F32),
            pltpu.VMEM((4, 4, 16, 1024), BF16),
            pltpu.VMEM((2048, 256), BF16),
            pltpu.VMEM((2, 128, 128), F32),
            pltpu.VMEM((128, 128), F32),
            pltpu.VMEM((4, 4, 2, 128, 128), BF16),
            pltpu.VMEM((8, 1, 128), F32),
            pltpu.VMEM((4, 1, 128), F32),
            pltpu.VMEM((D, VOCAB_DEV), BF16),
            pltpu.VMEM((ROWS, VOCAB_DEV), F32),
            pltpu.VMEM((32, 1, 384), F32),
            dma((6,)),
            dma((4,)),
            dma((2,)),
            dma((1,)),
            dma((1,)),
            dma((2, 4)),
            dma((2, 16)),
            dma((2,)),
            dma((2,)),
            dma((1,)),
            dma((1,)),
            dma((2, 4)),
            dma((2, 16)),
            dma((16,)),
            dma((2,)),
            dma((1,)),
            dma((14,)),
        ],
        compiler_params=pltpu.CompilerParams(
            collective_id=0, has_side_effects=True, vmem_limit_bytes=56 * 1024 * 1024
        ),
        name="score_response",
    )(
        queries, response_keys, response_values, prompt_keys, prompt_values, resp_len, residual,
        out_weight, norm_gain.reshape(1, 128), vocab_weight, targets.reshape(1, ROWS),
    )
    layer_out, row_loss = pl.pallas_call(
        hand_over, out_shape=shapes, in_specs=[vmem, vmem], out_specs=(vmem, vmem), name="hand_over"
    )(*results)
    return layer_out, row_loss.reshape(ROWS)


def solution(mesh):
    placed = (
        P(("batch", "seq"), None),
        P(("batch", "seq"), None),
        P(("batch", "seq"), None),
        P(("batch", "seq"), None),
        P(("batch", "seq"), None),
        P("batch"),
        P("batch", "seq"),
        P(None, "seq"),
        P("seq"),
        P(None, "seq"),
        P("batch"),
    )
    return jax.shard_map(
        local,
        mesh=mesh,
        in_specs=placed,
        out_specs=(P("batch", "seq"), P("batch")),
        check_vma=False,
    )
```

```python
import functools

import jax
import jax.numpy as jnp
from jax import lax
from jax.experimental import pallas as pl
from jax.experimental.pallas import tpu as pltpu
from jax.sharding import PartitionSpec as P

D = 4096
KEY_VALUE_HEADS = 4
HEAD_SIZE = 128
ROWS = 128
VOCAB_DEV = 2432
KEYS_DEV = 1024
LOG2E = 1.4426950408889634
SCORE_SCALE = LOG2E * HEAD_SIZE ** (-0.5)
MESH = pl.DeviceIdType.MESH
F32 = jnp.float32
BF16 = jnp.bfloat16


def dot_nt(a, b):
    return lax.dot_general(a, b, (((1,), (1,)), ((), ())), preferred_element_type=F32)


def dot_nn(a, b):
    return jnp.dot(a, b, preferred_element_type=F32)


def eye_mask():
    return lax.broadcasted_iota(jnp.int32, (128, 128), 0) == lax.broadcasted_iota(
        jnp.int32, (128, 128), 1
    )


def to_row(column):
    return jnp.sum(jnp.where(eye_mask(), column, 0.0), axis=0, keepdims=True)


def to_column(row):
    return jnp.sum(jnp.where(eye_mask(), row, 0.0), axis=1, keepdims=True)


def drain(ref, sem):
    pltpu.make_async_copy(ref, ref, sem).wait()


def kernel(
    queries, response_keys, response_values, prompt_keys, prompt_values, length, residual_in,
    out_weight, gain_in, vocab_weight, targets_in,
    layer_out, row_loss,
    residual, gain, targets, spread, small, resp, respbuf, kbuf, kt, vbuf, qbuf, ostage, sstage, rbuf, rstat, mrg, abuf, wbuf,
    pown, ppart, gbuf, ssbuf, ssplane, wv, acc, fbuf,
    local_sem, vocab_sem, kv_recv, w_recv, small_recv, q_ring, q_diag, r_recv, own_sem, a_recv,
    p_recv, g_ring, g_diag, h_recv, s_recv, f_recv, send_sem,
):
    me = lax.axis_index("seq")
    z, x, c = me // 8, (me // 2) % 4, me % 2
    chip = me // 2
    other = 1 - c
    sibling = chip * 2 + other

    def turn(a, d):
        return lax.rem(a + d, 4)

    def device(cz, cx, core):
        return (cz * 4 + cx) * 2 + core

    def send(src, dst, sem, target, kind):
        pltpu.make_async_remote_copy(
            src_ref=src, dst_ref=dst, send_sem=send_sem.at[kind], recv_sem=sem,
            device_id={"seq": target}, device_id_type=MESH,
        ).start()

    my_cols = pl.ds(pl.multiple_of(c * 256, 256), 256)
    other_cols = pl.ds(pl.multiple_of(other * 256, 256), 256)
    my_half = pl.ds(pl.multiple_of(c * 2048, 2048), 2048)
    other_half = pl.ds(pl.multiple_of(other * 2048, 2048), 2048)
    w_lane = pl.ds(pl.multiple_of(c * 128, 128), 128)

    barrier = pltpu.get_barrier_semaphore()
    x_peers = [device(z, turn(x, d), core) for d in (2, 1, 3) for core in (c, other)]
    z_peers = [device(turn(z, d), x, core) for d in (2, 1, 3) for core in (c, other)]
    for peer in z_peers + x_peers + [sibling]:
        pl.semaphore_signal(barrier, inc=1, device_id={"seq": peer}, device_id_type=MESH)

    own_copies = [
        pltpu.make_async_copy(prompt_keys.at[:, my_cols], kbuf.at[c], local_sem.at[0]),
        pltpu.make_async_copy(out_weight.at[my_half, :], wbuf.at[:, w_lane], local_sem.at[1]),
        pltpu.make_async_copy(residual_in, residual, local_sem.at[3]),
        pltpu.make_async_copy(gain_in, gain, local_sem.at[4]),
        pltpu.make_async_copy(targets_in, targets, local_sem.at[5]),
    ]
    value_copies = [
        pltpu.make_async_copy(
            prompt_values.at[:, pl.ds(pl.multiple_of(c * 256 + j * 128, 128), 128)],
            vbuf.at[j, c, :, pl.ds(0, 128)], local_sem.at[6 + j],
        )
        for j in range(2)
    ]
    for copy in own_copies + value_copies:
        copy.start()
    vbuf[:, :, :, 128:] = jnp.ones((2, 2, KEYS_DEV, 128), BF16)
    vocab_copies = [
        pltpu.make_async_copy(
            vocab_weight.at[pl.ds(i * 1024, 1024), :], wv.at[pl.ds(i * 1024, 1024), :],
            vocab_sem.at[i],
        )
        for i in range(4)
    ]

    wide = queries[...].astype(F32)
    for head in range(32):
        spread[head // 8, pl.ds(head % 8, 4, stride=8), :] = wide[:, head * 128 : head * 128 + 128]
    nothing = jnp.zeros((12, 128), F32)
    for g in range(4):
        cols = slice(g * 128, g * 128 + 128)
        small[g] = spread[g].astype(BF16)
        resp[g, 0:16, :] = jnp.concatenate([response_keys[:, cols].astype(F32), nothing], 0).astype(BF16)
        resp[g, 16:32, :] = jnp.concatenate([response_values[:, cols].astype(F32), nothing], 0).astype(BF16)
    q_rows = pl.ds(pl.multiple_of((x * 2 + c) * 32, 32), 32)
    my_heads, other_heads = pl.ds(2 * c, 2), pl.ds(2 * other, 2)
    for j in range(2):
        qbuf[z, j, q_rows, :] = small[2 * c + j]
        respbuf[c, j] = resp[2 * c + j]

    pl.semaphore_wait(barrier, 13)

    send(resp.at[other_heads], respbuf.at[c], small_recv.at[0], sibling, 1)
    def q_half(cz, cx, part):
        return qbuf.at[cz, part, pl.ds(pl.multiple_of(cx * 64, 64), 64), :]

    mine = qbuf.at[z, :, q_rows, :]
    send(small.at[other_heads], mine, q_ring.at[0, 0], sibling, 0)
    for d in (1, 3, 2):
        for core in (c, other):
            heads = small.at[pl.ds(2 * core, 2)]
            send(heads, mine, q_ring.at[0, 4 - d], device(z, turn(x, d), core), 0)
            send(heads, mine, q_ring.at[1, 4 - d], device(turn(z, d), x, core), 0)
    send(prompt_keys.at[:, other_cols], kbuf.at[c], kv_recv.at[0], sibling, 2)
    for j in range(2):
        send(
            prompt_values.at[:, pl.ds(pl.multiple_of(other * 256 + j * 128, 128), 128)],
            vbuf.at[j, c, :, pl.ds(0, 128)], kv_recv.at[1 + j], sibling, 2,
        )

    def turn_keys(core):
        for j in range(2):
            kt[j, core] = kbuf[core, :, j * 128 : (j + 1) * 128].T

    own_copies[0].wait()
    turn_keys(c)
    for d in (1, 3, 2):
        sx, sz = turn(x, d), turn(z, d)
        drain(qbuf.at[0, 0, pl.ds(0, 128), :], q_ring.at[0, d])
        for e in (1, 3, 2):
            block = q_half(z, sx, 0)
            send(block, block, q_diag.at[0, (4 - e) * 4 + d], device(turn(z, e), x, c), 12)
        drain(qbuf.at[0, 0, pl.ds(0, 128), :], q_ring.at[1, d])
        for e in (1, 3, 2):
            block = q_half(sz, x, 1)
            send(block, block, q_diag.at[1, d * 4 + 4 - e], device(z, turn(x, e), c), 12)
    drain(qbuf.at[0, 0, pl.ds(0, 64), :], q_ring.at[0, 0])
    send(out_weight.at[other_half, :], wbuf.at[:, w_lane], w_recv.at[0], sibling, 3)
    for copy in vocab_copies:
        copy.start()

    live = length[0]
    key_column = lax.broadcasted_iota(jnp.int32, (256, 32), 1)
    key_id = chip * 8 + (key_column // 16) * 4 + key_column % 16
    key_ok = (key_column % 16 < 4) & (key_id < live)
    row_in_plane = lax.broadcasted_iota(jnp.int32, (256, 32), 0) // 8
    drain(resp.at[pl.ds(0, 2)], small_recv.at[0])
    drain(kbuf.at[0], kv_recv.at[0])
    turn_keys(other)
    for j in range(2):
        value_copies[j].wait()
        drain(vbuf.at[0, 0, :, pl.ds(0, 128)], kv_recv.at[1 + j])

    def with_ones(v):
        return jnp.concatenate([v, jnp.ones_like(v)], 1)

    for u, offset in enumerate((0, 1 + 2 * (x % 2), 2, 3 - 2 * (x % 2))):
        t = turn(z, offset)
        if u > 0:
            for dx in (1, 3, 2):
                for part in range(2):
                    drain(qbuf.at[0, 0, pl.ds(0, 64), :], q_diag.at[part, offset * 4 + dx])

        visible = key_ok & (key_id <= t * 32 + row_in_plane)
        for j in range(2):
            q = qbuf[t, j]
            s0 = dot_nn(q, kt[j, 0])
            s1 = dot_nn(q, kt[j, 1])
            resp_keys = jnp.concatenate([respbuf[0, j, 0:16, :], respbuf[1, j, 0:16, :]], 0)
            resp_values = jnp.concatenate([respbuf[0, j, 16:32, :], respbuf[1, j, 16:32, :]], 0)
            sr = jnp.where(visible, dot_nt(q, resp_keys), -jnp.inf)
            peak = jnp.maximum(
                jnp.maximum(jnp.max(s0, 1, keepdims=True), jnp.max(s1, 1, keepdims=True)),
                jnp.max(sr, 1, keepdims=True),
            ) * SCORE_SCALE
            p0 = jnp.exp2(s0 * SCORE_SCALE - peak)
            p1 = jnp.exp2(s1 * SCORE_SCALE - peak)
            pr = jnp.exp2(sr * SCORE_SCALE - peak)
            o = (
                dot_nn(p0.astype(BF16), vbuf[j, 0])
                + dot_nn(p1.astype(BF16), vbuf[j, 1])
                + dot_nn(pr.astype(BF16), with_ones(resp_values))
            )
            total = o[:, 128:]
            ostage[u, j] = o[:, :128].astype(BF16)
            for half in range(2):
                rows = slice(half * 128, (half + 1) * 128)
                sstage[u, j, half, 0:1, :] = to_row(peak[rows])
                sstage[u, j, half, 1:2, :] = to_row(total[rows])
        for quarter in range(4):
            half, j = quarter // 2, quarter % 2
            owner = device(t, quarter, c)
            part = ostage.at[u, j, pl.ds(half * 128, 128), :]
            stat = sstage.at[u, j, half]

            def to_owner():
                send(part, rbuf.at[chip], r_recv.at[0], owner, 4)
                send(stat, rstat.at[chip], r_recv.at[1], owner, 5)

            if u > 0:
                to_owner()
                continue
            pl.when(owner != me)(to_owner)

            @pl.when(owner == me)
            def _():
                pltpu.make_async_copy(part, rbuf.at[chip], own_sem.at[0]).start()
                pltpu.make_async_copy(stat, rstat.at[chip], own_sem.at[1]).start()

    drain(rstat.at[pl.ds(0, 15)], r_recv.at[1])
    drain(rstat.at[0], own_sem.at[1])
    peaks = rstat[:, 0, :]
    weight = jnp.exp2(peaks - jnp.max(peaks, 0, keepdims=True))
    weight = weight / jnp.sum(weight * rstat[:, 1, :], 0, keepdims=True)
    weight = jnp.concatenate([weight, jnp.zeros((112, 128), F32)], 0).T
    drain(rbuf.at[pl.ds(0, 15)], r_recv.at[0])
    drain(rbuf.at[0], own_sem.at[0])
    merged = weight[:, 0:1] * rbuf[0].astype(F32)
    for k in range(1, 16):
        merged += weight[:, k : k + 1] * rbuf[k].astype(F32)
    mrg[...] = merged
    block = jnp.concatenate([mrg[pl.ds(h, 16, stride=8), :] for h in range(8)], 1)
    abuf[z, x] = block.astype(BF16)

    def torus_distance(d):
        return min(d[0], 4 - d[0]) + min(d[1], 4 - d[1])

    far_first = sorted([(dz, dx) for dz in range(4) for dx in range(4)], key=lambda d: -torus_distance(d))
    for dz, dx in far_first[:-1]:
        send(abuf.at[z, x], abuf.at[z, x], a_recv.at[0], device(turn(z, dz), turn(x, dx), c), 6)
    for copy in own_copies[1:]:
        copy.wait()
    drain(wbuf.at[:, pl.ds(0, 128)], w_recv.at[0])
    drain(rbuf.at[pl.ds(0, 15)], a_recv.at[0])
    projected = None
    for j in range(2):
        attn = jnp.concatenate(
            [abuf[t, 2 * half + j] for t in range(4) for half in range(2)], 0
        )
        term = dot_nn(attn, wbuf[pl.ds(j * 1024, 1024), :])
        projected = term if j == 0 else projected + term
    pown[0] = projected[:, :128]
    pown[1] = projected[:, 128:]
    send(pown.at[other], ppart, p_recv.at[0], sibling, 7)
    base = residual[...].astype(F32) + pown[c]
    drain(ppart, p_recv.at[0])
    layer = (base + ppart[...]).astype(BF16)
    layer_out[...] = layer
    layer = layer.astype(F32)
    gbuf[z, x, c] = (layer * gain[...]).astype(BF16)
    ssbuf[x * 2 + c] = to_row(jnp.sum(layer * layer, 1, keepdims=True))

    def gather(full, half, ring, diag, kind, first_sent, on_ring):
        for d in (1, 3, 2):
            send(full(z, x), full(z, x), ring.at[0, 4 - d], device(z, turn(x, d), c), kind)
            send(full(z, x), full(z, x), ring.at[1, 4 - d], device(turn(z, d), x, c), kind)
        first_sent()
        for d in (1, 3, 2):
            sx, sz = turn(x, d), turn(z, d)
            drain(full(0, 0), ring.at[0, d])
            for e in (1, 3, 2):
                block = half(z, sx, 0)
                send(block, block, diag.at[0, (4 - e) * 4 + d], device(turn(z, e), x, c), kind)
            on_ring(z, sx, d)
            drain(full(0, 0), ring.at[1, d])
            for e in (1, 3, 2):
                block = half(sz, x, 1)
                send(block, block, diag.at[1, d * 4 + 4 - e], device(z, turn(x, e), c), kind)
            on_ring(sz, x, d * 4)

    def g_full(cz, cx):
        return gbuf.at[cz, cx, c]

    def g_half(cz, cx, part):
        return gbuf.at[cz, cx, c, pl.ds(part * 64, 64), :]

    def to_sibling(cz, cx, index):
        send(g_full(cz, cx), g_full(cz, cx), h_recv.at[index], sibling, 9)

    def first_sent():
        to_sibling(z, x, 0)
        for peer in x_peers + [sibling]:
            mine = ssbuf.at[x * 2 + c]
            send(mine, mine, s_recv.at[0], peer, 10)

    gather(g_full, g_half, g_ring, g_diag, 8, first_sent, to_sibling)
    drain(ssbuf.at[pl.ds(0, 7)], s_recv.at[0])
    ssplane[z] = jnp.sum(ssbuf[:, 0, :], 0, keepdims=True)
    for d in (2, 1, 3):
        send(ssplane.at[z], ssplane.at[z], s_recv.at[1], device(turn(z, d), x, c), 11)

    def plane_features(cz):
        return jnp.concatenate([gbuf[cz, cx, core] for cx in range(4) for core in range(2)], 1)

    def plane_rows(cz):
        return pl.ds(pl.multiple_of(cz * 1024, 1024), 1024)

    for copy in vocab_copies:
        copy.wait()
    for dx in range(4):
        drain(gbuf.at[0, 0, 0], h_recv.at[dx])
    acc[...] = dot_nn(plane_features(z), wv[plane_rows(z), :])
    for dz in (1, 3, 2):
        for dx in (1, 3, 2):
            for part in range(2):
                drain(g_half(0, 0, part), g_diag.at[part, dz * 4 + dx])
            to_sibling(turn(z, dz), turn(x, dx), dz * 4 + dx)
    for dz in (1, 3, 2):
        for dx in range(4):
            drain(gbuf.at[0, 0, 0], h_recv.at[dz * 4 + dx])
    planes = [turn(z, dz) for dz in (1, 2, 3)]
    features = [plane_features(cz) for cz in planes]
    for n in range(0, VOCAB_DEV, 512):
        cols = slice(n, min(n + 512, VOCAB_DEV))
        part = acc[:, cols]
        for cz, f in zip(planes, features):
            part += dot_nn(f, wv[plane_rows(cz), cols])
        acc[:, cols] = part

    drain(ssplane.at[pl.ds(0, 3)], s_recv.at[1])
    squares = jnp.sum(ssplane[:, 0, :], 0, keepdims=True)
    inverse = to_column(lax.rsqrt(squares / D + 1e-06))
    logits = acc[...] * inverse
    top = jnp.max(logits, 1, keepdims=True)
    exp_total = jnp.sum(jnp.exp(logits - top), 1, keepdims=True)
    target = to_column(targets[...].astype(F32)).astype(jnp.int32) - me * VOCAB_DEV
    hit = lax.broadcasted_iota(jnp.int32, (ROWS, VOCAB_DEV), 1) == target
    target_logit = jnp.sum(jnp.where(hit, logits, 0.0), 1, keepdims=True)
    fbuf[me] = jnp.concatenate([to_row(top), to_row(exp_total), to_row(target_logit)], 1)

    for dz, dx in far_first:
        for core in (c, other):
            if (dz, dx) != (0, 0) or core is other:
                target_device = device(turn(z, dz), turn(x, dx), core)
                send(fbuf.at[me], fbuf.at[me], f_recv.at[0], target_device, 13)
    drain(fbuf.at[pl.ds(0, 31)], f_recv.at[0])
    tops = fbuf[:, 0, 0:128]
    top = jnp.max(tops, 0, keepdims=True)
    whole = jnp.sum(fbuf[:, 0, 128:256] * jnp.exp(tops - top), 0, keepdims=True)
    loss = top + jnp.log(whole) - jnp.sum(fbuf[:, 0, 256:384], 0, keepdims=True)
    row_ids = lax.broadcasted_iota(jnp.int32, (1, ROWS), 1)
    row_loss[...] = jnp.where(row_ids < live, loss, 0.0)

    drain(kbuf.at[0, pl.ds(0, 416), :], send_sem.at[0])
    drain(resp.at[pl.ds(0, 2)], send_sem.at[1])
    drain(kbuf, send_sem.at[2])
    drain(wbuf.at[:, pl.ds(0, 128)], send_sem.at[3])
    drain(rbuf.at[pl.ds(0, 15)], send_sem.at[4])
    drain(rstat.at[pl.ds(0, 15)], send_sem.at[5])
    drain(rbuf.at[pl.ds(0, 15)], send_sem.at[6])
    drain(ppart, send_sem.at[7])
    drain(rbuf.at[pl.ds(0, 15)], send_sem.at[8])
    drain(rbuf, send_sem.at[9])
    drain(ssbuf.at[pl.ds(0, 7)], send_sem.at[10])
    drain(ssplane.at[pl.ds(0, 3)], send_sem.at[11])
    drain(kbuf.at[0, pl.ds(0, 576), :], send_sem.at[12])
    drain(fbuf.at[pl.ds(0, 31)], send_sem.at[13])


def hand_over(layer, loss, layer_out, loss_out):
    layer_out[...] = layer[...]
    loss_out[...] = loss[...]


def local(
    queries, prompt_keys, prompt_values, response_keys, response_values, resp_len, residual,
    out_weight, norm_gain, vocab_weight, targets,
):
    vmem = pl.BlockSpec(memory_space=pltpu.VMEM)
    hbm = pl.BlockSpec(memory_space=pl.ANY)
    dma = pltpu.SemaphoreType.DMA
    shapes = (
        jax.ShapeDtypeStruct((ROWS, 128), BF16),
        jax.ShapeDtypeStruct((1, ROWS), F32),
    )
    results = pl.pallas_call(
        kernel,
        out_shape=shapes,
        in_specs=[
            vmem, vmem, vmem, hbm, hbm, pl.BlockSpec(memory_space=pltpu.SMEM), hbm, hbm, hbm,
            hbm, hbm,
        ],
        out_specs=(vmem, vmem),
        scratch_shapes=[
            pltpu.VMEM((ROWS, 128), BF16),
            pltpu.VMEM((1, 128), F32),
            pltpu.VMEM((1, ROWS), jnp.int32),
            pltpu.VMEM((4, 32, 128), F32),
            pltpu.VMEM((4, 32, 128), BF16),
            pltpu.VMEM((4, 32, 128), BF16),
            pltpu.VMEM((2, 2, 32, 128), BF16),
            pltpu.VMEM((2, KEYS_DEV, 256), BF16),
            pltpu.VMEM((2, 2, 128, KEYS_DEV), BF16),
            pltpu.VMEM((2, 2, KEYS_DEV, 256), BF16),
            pltpu.VMEM((4, 2, 256, 128), BF16),
            pltpu.VMEM((4, 2, 256, 128), BF16),
            pltpu.VMEM((4, 2, 2, 8, 128), F32),
            pltpu.VMEM((16, 128, 128), BF16),
            pltpu.VMEM((16, 8, 128), F32),
            pltpu.VMEM((128, 128), F32),
            pltpu.VMEM((4, 4, 16, 1024), BF16),
            pltpu.VMEM((2048, 256), BF16),
            pltpu.VMEM((2, 128, 128), F32),
            pltpu.VMEM((128, 128), F32),
            pltpu.VMEM((4, 4, 2, 128, 128), BF16),
            pltpu.VMEM((8, 1, 128), F32),
            pltpu.VMEM((4, 1, 128), F32),
            pltpu.VMEM((D, VOCAB_DEV), BF16),
            pltpu.VMEM((ROWS, VOCAB_DEV), F32),
            pltpu.VMEM((32, 1, 384), F32),
            dma((8,)),
            dma((4,)),
            dma((3,)),
            dma((1,)),
            dma((1,)),
            dma((2, 4)),
            dma((2, 16)),
            dma((2,)),
            dma((2,)),
            dma((1,)),
            dma((1,)),
            dma((2, 4)),
            dma((2, 16)),
            dma((16,)),
            dma((2,)),
            dma((1,)),
            dma((14,)),
        ],
        compiler_params=pltpu.CompilerParams(
            collective_id=0, has_side_effects=True, vmem_limit_bytes=56 * 1024 * 1024
        ),
        name="score_response",
    )(
        queries, response_keys, response_values, prompt_keys, prompt_values, resp_len, residual,
        out_weight, norm_gain.reshape(1, 128), vocab_weight, targets.reshape(1, ROWS),
    )
    layer_out, row_loss = pl.pallas_call(
        hand_over, out_shape=shapes, in_specs=[vmem, vmem], out_specs=(vmem, vmem), name="hand_over"
    )(*results)
    return layer_out, row_loss.reshape(ROWS)


def solution(mesh):
    placed = (
        P(("batch", "seq"), None),
        P(("batch", "seq"), None),
        P(("batch", "seq"), None),
        P(("batch", "seq"), None),
        P(("batch", "seq"), None),
        P("batch"),
        P("batch", "seq"),
        P(None, "seq"),
        P("seq"),
        P(None, "seq"),
        P("batch"),
    )
    return jax.shard_map(
        local,
        mesh=mesh,
        in_specs=placed,
        out_specs=(P("batch", "seq"), P("batch")),
        check_vma=False,
    )
```

```python
import functools

import jax
import jax.numpy as jnp
from jax import lax
from jax.experimental import pallas as pl
from jax.experimental.pallas import tpu as pltpu
from jax.sharding import PartitionSpec as P

D = 4096
KEY_VALUE_HEADS = 4
HEAD_SIZE = 128
ROWS = 128
VOCAB_DEV = 2432
KEYS_DEV = 1024
LOG2E = 1.4426950408889634
SCORE_SCALE = LOG2E * HEAD_SIZE ** (-0.5)
MESH = pl.DeviceIdType.MESH
F32 = jnp.float32
BF16 = jnp.bfloat16


def dot_nt(a, b):
    return lax.dot_general(a, b, (((1,), (1,)), ((), ())), preferred_element_type=F32)


def dot_nn(a, b):
    return jnp.dot(a, b, preferred_element_type=F32)


def eye_mask():
    return lax.broadcasted_iota(jnp.int32, (128, 128), 0) == lax.broadcasted_iota(
        jnp.int32, (128, 128), 1
    )


def to_row(column):
    return jnp.sum(jnp.where(eye_mask(), column, 0.0), axis=0, keepdims=True)


def to_column(row):
    return jnp.sum(jnp.where(eye_mask(), row, 0.0), axis=1, keepdims=True)


def drain(ref, sem):
    pltpu.make_async_copy(ref, ref, sem).wait()


def kernel(
    queries, response_keys, response_values, prompt_keys, prompt_values, length, residual_in,
    out_weight, gain_in, vocab_weight, targets_in,
    layer_out, row_loss,
    residual, gain, targets, spread, small, resp, respbuf, kbuf, kt, vbuf, qbuf, ostage, sstage, rbuf, rstat, mrg, abuf, wbuf,
    pown, ppart, gbuf, ssbuf, ssplane, wv, acc, fbuf,
    local_sem, vocab_sem, kv_recv, w_recv, small_recv, q_ring, q_diag, r_recv, own_sem, a_recv,
    p_recv, g_ring, g_diag, h_recv, s_recv, f_recv, send_sem,
):
    me = lax.axis_index("seq")
    z, x, c = me // 8, (me // 2) % 4, me % 2
    chip = me // 2
    other = 1 - c
    sibling = chip * 2 + other

    def turn(a, d):
        return lax.rem(a + d, 4)

    def device(cz, cx, core):
        return (cz * 4 + cx) * 2 + core

    def send(src, dst, sem, target, kind):
        pltpu.make_async_remote_copy(
            src_ref=src, dst_ref=dst, send_sem=send_sem.at[kind], recv_sem=sem,
            device_id={"seq": target}, device_id_type=MESH,
        ).start()

    my_cols = pl.ds(pl.multiple_of(c * 256, 256), 256)
    other_cols = pl.ds(pl.multiple_of(other * 256, 256), 256)
    my_half = pl.ds(pl.multiple_of(c * 2048, 2048), 2048)
    other_half = pl.ds(pl.multiple_of(other * 2048, 2048), 2048)
    w_lane = pl.ds(pl.multiple_of(c * 128, 128), 128)

    barrier = pltpu.get_barrier_semaphore()
    x_peers = [device(z, turn(x, d), core) for d in (2, 1, 3) for core in (c, other)]
    z_peers = [device(turn(z, d), x, core) for d in (2, 1, 3) for core in (c, other)]
    for peer in z_peers + x_peers + [sibling]:
        pl.semaphore_signal(barrier, inc=1, device_id={"seq": peer}, device_id_type=MESH)

    own_copies = [
        pltpu.make_async_copy(prompt_keys.at[:, my_cols], kbuf.at[c], local_sem.at[0]),
        pltpu.make_async_copy(out_weight.at[my_half, :], wbuf.at[:, w_lane], local_sem.at[1]),
        pltpu.make_async_copy(residual_in, residual, local_sem.at[3]),
        pltpu.make_async_copy(gain_in, gain, local_sem.at[4]),
        pltpu.make_async_copy(targets_in, targets, local_sem.at[5]),
    ]
    value_copies = [
        pltpu.make_async_copy(
            prompt_values.at[:, pl.ds(pl.multiple_of(c * 256 + j * 128, 128), 128)],
            vbuf.at[j, c, :, pl.ds(0, 128)], local_sem.at[6 + j],
        )
        for j in range(2)
    ]
    for copy in own_copies + value_copies:
        copy.start()
    vbuf[:, :, :, 128:] = jnp.ones((2, 2, KEYS_DEV, 128), BF16)
    vocab_copies = [
        pltpu.make_async_copy(
            vocab_weight.at[pl.ds(i * 1024, 1024), :], wv.at[pl.ds(i * 1024, 1024), :],
            vocab_sem.at[i],
        )
        for i in range(4)
    ]

    wide = queries[...].astype(F32)
    for head in range(32):
        spread[head // 8, pl.ds(head % 8, 4, stride=8), :] = wide[:, head * 128 : head * 128 + 128]
    nothing = jnp.zeros((12, 128), F32)
    for g in range(4):
        cols = slice(g * 128, g * 128 + 128)
        small[g] = spread[g].astype(BF16)
        resp[g, 0:16, :] = jnp.concatenate([response_keys[:, cols].astype(F32), nothing], 0).astype(BF16)
        resp[g, 16:32, :] = jnp.concatenate([response_values[:, cols].astype(F32), nothing], 0).astype(BF16)
    q_rows = pl.ds(pl.multiple_of((x * 2 + c) * 32, 32), 32)
    my_heads, other_heads = pl.ds(2 * c, 2), pl.ds(2 * other, 2)
    for j in range(2):
        qbuf[z, j, q_rows, :] = small[2 * c + j]
        respbuf[c, j] = resp[2 * c + j]

    pl.semaphore_wait(barrier, 13)

    send(resp.at[other_heads], respbuf.at[c], small_recv.at[0], sibling, 1)
    def q_half(cz, cx, part):
        return qbuf.at[cz, part, pl.ds(pl.multiple_of(cx * 64, 64), 64), :]

    mine = qbuf.at[z, :, q_rows, :]
    send(small.at[other_heads], mine, q_ring.at[0, 0], sibling, 0)
    for d in (1, 3, 2):
        for core in (c, other):
            heads = small.at[pl.ds(2 * core, 2)]
            send(heads, mine, q_ring.at[0, 4 - d], device(z, turn(x, d), core), 0)
            send(heads, mine, q_ring.at[1, 4 - d], device(turn(z, d), x, core), 0)
    send(prompt_keys.at[:, other_cols], kbuf.at[c], kv_recv.at[0], sibling, 2)
    for j in range(2):
        send(
            prompt_values.at[:, pl.ds(pl.multiple_of(other * 256 + j * 128, 128), 128)],
            vbuf.at[j, c, :, pl.ds(0, 128)], kv_recv.at[1 + j], sibling, 2,
        )

    def turn_keys(core):
        for j in range(2):
            kt[j, core] = kbuf[core, :, j * 128 : (j + 1) * 128].T

    own_copies[0].wait()
    turn_keys(c)
    for d in (1, 3, 2):
        sx, sz = turn(x, d), turn(z, d)
        drain(qbuf.at[0, 0, pl.ds(0, 128), :], q_ring.at[0, d])
        for e in (1, 3, 2):
            block = q_half(z, sx, 0)
            send(block, block, q_diag.at[0, (4 - e) * 4 + d], device(turn(z, e), x, c), 12)
        drain(qbuf.at[0, 0, pl.ds(0, 128), :], q_ring.at[1, d])
        for e in (1, 3, 2):
            block = q_half(sz, x, 1)
            send(block, block, q_diag.at[1, d * 4 + 4 - e], device(z, turn(x, e), c), 12)
    drain(qbuf.at[0, 0, pl.ds(0, 64), :], q_ring.at[0, 0])
    send(out_weight.at[other_half, :], wbuf.at[:, w_lane], w_recv.at[0], sibling, 3)
    for copy in vocab_copies:
        copy.start()

    live = length[0]
    key_column = lax.broadcasted_iota(jnp.int32, (256, 32), 1)
    key_id = chip * 8 + (key_column // 16) * 4 + key_column % 16
    key_ok = (key_column % 16 < 4) & (key_id < live)
    row_in_plane = lax.broadcasted_iota(jnp.int32, (256, 32), 0) // 8
    drain(resp.at[pl.ds(0, 2)], small_recv.at[0])
    drain(kbuf.at[0], kv_recv.at[0])
    turn_keys(other)
    for j in range(2):
        value_copies[j].wait()
        drain(vbuf.at[0, 0, :, pl.ds(0, 128)], kv_recv.at[1 + j])

    def with_ones(v):
        return jnp.concatenate([v, jnp.ones_like(v)], 1)

    for u, offset in enumerate((0, 1 + 2 * (x % 2), 2, 3 - 2 * (x % 2))):
        t = turn(z, offset)
        if u > 0:
            for dx in (1, 3, 2):
                for part in range(2):
                    drain(qbuf.at[0, 0, pl.ds(0, 64), :], q_diag.at[part, offset * 4 + dx])

        visible = key_ok & (key_id <= t * 32 + row_in_plane)
        for j in range(2):
            q = qbuf[t, j]
            s0 = dot_nn(q, kt[j, 0])
            s1 = dot_nn(q, kt[j, 1])
            resp_keys = jnp.concatenate([respbuf[0, j, 0:16, :], respbuf[1, j, 0:16, :]], 0)
            resp_values = jnp.concatenate([respbuf[0, j, 16:32, :], respbuf[1, j, 16:32, :]], 0)
            sr = jnp.where(visible, dot_nt(q, resp_keys), -jnp.inf)
            peak = jnp.maximum(
                jnp.maximum(jnp.max(s0, 1, keepdims=True), jnp.max(s1, 1, keepdims=True)),
                jnp.max(sr, 1, keepdims=True),
            ) * SCORE_SCALE
            p0 = jnp.exp2(s0 * SCORE_SCALE - peak)
            p1 = jnp.exp2(s1 * SCORE_SCALE - peak)
            pr = jnp.exp2(sr * SCORE_SCALE - peak)
            o = (
                dot_nn(p0.astype(BF16), vbuf[j, 0])
                + dot_nn(p1.astype(BF16), vbuf[j, 1])
                + dot_nn(pr.astype(BF16), with_ones(resp_values))
            )
            total = o[:, 128:]
            ostage[u, j] = o[:, :128].astype(BF16)
            for half in range(2):
                rows = slice(half * 128, (half + 1) * 128)
                sstage[u, j, half, 0:1, :] = to_row(peak[rows])
                sstage[u, j, half, 1:2, :] = to_row(total[rows])
        for quarter in range(4):
            half, j = quarter // 2, quarter % 2
            owner = device(t, quarter, c)
            part = ostage.at[u, j, pl.ds(half * 128, 128), :]
            stat = sstage.at[u, j, half]

            def to_owner():
                send(part, rbuf.at[chip], r_recv.at[0], owner, 4)
                send(stat, rstat.at[chip], r_recv.at[1], owner, 5)

            if u > 0:
                to_owner()
                continue
            pl.when(owner != me)(to_owner)

            @pl.when(owner == me)
            def _():
                pltpu.make_async_copy(part, rbuf.at[chip], own_sem.at[0]).start()
                pltpu.make_async_copy(stat, rstat.at[chip], own_sem.at[1]).start()

    drain(rstat.at[pl.ds(0, 15)], r_recv.at[1])
    drain(rstat.at[0], own_sem.at[1])
    peaks = rstat[:, 0, :]
    weight = jnp.exp2(peaks - jnp.max(peaks, 0, keepdims=True))
    weight = weight / jnp.sum(weight * rstat[:, 1, :], 0, keepdims=True)
    weight = jnp.concatenate([weight, jnp.zeros((112, 128), F32)], 0).T
    drain(rbuf.at[pl.ds(0, 15)], r_recv.at[0])
    drain(rbuf.at[0], own_sem.at[0])
    merged = weight[:, 0:1] * rbuf[0].astype(F32)
    for k in range(1, 16):
        merged += weight[:, k : k + 1] * rbuf[k].astype(F32)
    mrg[...] = merged
    block = jnp.concatenate([mrg[pl.ds(h, 16, stride=8), :] for h in range(8)], 1)
    abuf[z, x] = block.astype(BF16)

    def torus_distance(d):
        return min(d[0], 4 - d[0]) + min(d[1], 4 - d[1])

    far_first = sorted([(dz, dx) for dz in range(4) for dx in range(4)], key=lambda d: -torus_distance(d))
    for dz, dx in far_first[:-1]:
        send(abuf.at[z, x], abuf.at[z, x], a_recv.at[0], device(turn(z, dz), turn(x, dx), c), 6)
    for copy in own_copies[1:]:
        copy.wait()
    drain(wbuf.at[:, pl.ds(0, 128)], w_recv.at[0])
    drain(rbuf.at[pl.ds(0, 15)], a_recv.at[0])
    attn = [
        jnp.concatenate([abuf[t, 2 * half + j] for t in range(4) for half in range(2)], 0)
        for j in range(2)
    ]

    def project(columns):
        lanes = pl.ds(pl.multiple_of(columns * 128, 128), 128)
        return dot_nn(attn[0], wbuf[pl.ds(0, 1024), lanes]) + dot_nn(
            attn[1], wbuf[pl.ds(1024, 1024), lanes]
        )

    pown[other] = project(other)
    send(pown.at[other], ppart, p_recv.at[0], sibling, 7)
    pown[c] = project(c)
    base = residual[...].astype(F32) + pown[c]
    drain(ppart, p_recv.at[0])
    layer = (base + ppart[...]).astype(BF16)
    layer_out[...] = layer
    layer = layer.astype(F32)
    gbuf[z, x, c] = (layer * gain[...]).astype(BF16)
    ssbuf[x * 2 + c] = to_row(jnp.sum(layer * layer, 1, keepdims=True))

    def gather(full, half, ring, diag, kind, first_sent, on_ring):
        for d in (1, 3, 2):
            send(full(z, x), full(z, x), ring.at[0, 4 - d], device(z, turn(x, d), c), kind)
            send(full(z, x), full(z, x), ring.at[1, 4 - d], device(turn(z, d), x, c), kind)
        first_sent()
        for d in (1, 3, 2):
            sx, sz = turn(x, d), turn(z, d)
            drain(full(0, 0), ring.at[0, d])
            for e in (1, 3, 2):
                block = half(z, sx, 0)
                send(block, block, diag.at[0, (4 - e) * 4 + d], device(turn(z, e), x, c), kind)
            on_ring(z, sx, d)
            drain(full(0, 0), ring.at[1, d])
            for e in (1, 3, 2):
                block = half(sz, x, 1)
                send(block, block, diag.at[1, d * 4 + 4 - e], device(z, turn(x, e), c), kind)
            on_ring(sz, x, d * 4)

    def g_full(cz, cx):
        return gbuf.at[cz, cx, c]

    def g_half(cz, cx, part):
        return gbuf.at[cz, cx, c, pl.ds(part * 64, 64), :]

    def to_sibling(cz, cx, index):
        send(g_full(cz, cx), g_full(cz, cx), h_recv.at[index], sibling, 9)

    def first_sent():
        to_sibling(z, x, 0)
        for peer in x_peers + [sibling]:
            mine = ssbuf.at[x * 2 + c]
            send(mine, mine, s_recv.at[0], peer, 10)

    gather(g_full, g_half, g_ring, g_diag, 8, first_sent, to_sibling)
    drain(ssbuf.at[pl.ds(0, 7)], s_recv.at[0])
    ssplane[z] = jnp.sum(ssbuf[:, 0, :], 0, keepdims=True)
    for d in (2, 1, 3):
        send(ssplane.at[z], ssplane.at[z], s_recv.at[1], device(turn(z, d), x, c), 11)

    def plane_features(cz):
        return jnp.concatenate([gbuf[cz, cx, core] for cx in range(4) for core in range(2)], 1)

    def plane_rows(cz):
        return pl.ds(pl.multiple_of(cz * 1024, 1024), 1024)

    for copy in vocab_copies:
        copy.wait()
    for dx in range(4):
        drain(gbuf.at[0, 0, 0], h_recv.at[dx])
    acc[...] = dot_nn(plane_features(z), wv[plane_rows(z), :])
    for dz in (1, 3, 2):
        for dx in (1, 3, 2):
            for part in range(2):
                drain(g_half(0, 0, part), g_diag.at[part, dz * 4 + dx])
            to_sibling(turn(z, dz), turn(x, dx), dz * 4 + dx)
    for dz in (1, 3, 2):
        for dx in range(4):
            drain(gbuf.at[0, 0, 0], h_recv.at[dz * 4 + dx])
    planes = [turn(z, dz) for dz in (1, 2, 3)]
    features = [plane_features(cz) for cz in planes]
    for n in range(0, VOCAB_DEV, 512):
        cols = slice(n, min(n + 512, VOCAB_DEV))
        part = acc[:, cols]
        for cz, f in zip(planes, features):
            part += dot_nn(f, wv[plane_rows(cz), cols])
        acc[:, cols] = part

    drain(ssplane.at[pl.ds(0, 3)], s_recv.at[1])
    squares = jnp.sum(ssplane[:, 0, :], 0, keepdims=True)
    inverse = to_column(lax.rsqrt(squares / D + 1e-06))
    logits = acc[...] * inverse
    top = jnp.max(logits, 1, keepdims=True)
    exp_total = jnp.sum(jnp.exp(logits - top), 1, keepdims=True)
    target = to_column(targets[...].astype(F32)).astype(jnp.int32) - me * VOCAB_DEV
    hit = lax.broadcasted_iota(jnp.int32, (ROWS, VOCAB_DEV), 1) == target
    target_logit = jnp.sum(jnp.where(hit, logits, 0.0), 1, keepdims=True)
    fbuf[me] = jnp.concatenate([to_row(top), to_row(exp_total), to_row(target_logit)], 1)

    for dz, dx in far_first:
        for core in (c, other):
            if (dz, dx) != (0, 0) or core is other:
                target_device = device(turn(z, dz), turn(x, dx), core)
                send(fbuf.at[me], fbuf.at[me], f_recv.at[0], target_device, 13)
    drain(fbuf.at[pl.ds(0, 31)], f_recv.at[0])
    tops = fbuf[:, 0, 0:128]
    top = jnp.max(tops, 0, keepdims=True)
    whole = jnp.sum(fbuf[:, 0, 128:256] * jnp.exp(tops - top), 0, keepdims=True)
    loss = top + jnp.log(whole) - jnp.sum(fbuf[:, 0, 256:384], 0, keepdims=True)
    row_ids = lax.broadcasted_iota(jnp.int32, (1, ROWS), 1)
    row_loss[...] = jnp.where(row_ids < live, loss, 0.0)

    drain(kbuf.at[0, pl.ds(0, 416), :], send_sem.at[0])
    drain(resp.at[pl.ds(0, 2)], send_sem.at[1])
    drain(kbuf, send_sem.at[2])
    drain(wbuf.at[:, pl.ds(0, 128)], send_sem.at[3])
    drain(rbuf.at[pl.ds(0, 15)], send_sem.at[4])
    drain(rstat.at[pl.ds(0, 15)], send_sem.at[5])
    drain(rbuf.at[pl.ds(0, 15)], send_sem.at[6])
    drain(ppart, send_sem.at[7])
    drain(rbuf.at[pl.ds(0, 15)], send_sem.at[8])
    drain(rbuf, send_sem.at[9])
    drain(ssbuf.at[pl.ds(0, 7)], send_sem.at[10])
    drain(ssplane.at[pl.ds(0, 3)], send_sem.at[11])
    drain(kbuf.at[0, pl.ds(0, 576), :], send_sem.at[12])
    drain(fbuf.at[pl.ds(0, 31)], send_sem.at[13])


def hand_over(layer, loss, layer_out, loss_out):
    layer_out[...] = layer[...]
    loss_out[...] = loss[...]


def local(
    queries, prompt_keys, prompt_values, response_keys, response_values, resp_len, residual,
    out_weight, norm_gain, vocab_weight, targets,
):
    vmem = pl.BlockSpec(memory_space=pltpu.VMEM)
    hbm = pl.BlockSpec(memory_space=pl.ANY)
    dma = pltpu.SemaphoreType.DMA
    shapes = (
        jax.ShapeDtypeStruct((ROWS, 128), BF16),
        jax.ShapeDtypeStruct((1, ROWS), F32),
    )
    results = pl.pallas_call(
        kernel,
        out_shape=shapes,
        in_specs=[
            vmem, vmem, vmem, hbm, hbm, pl.BlockSpec(memory_space=pltpu.SMEM), hbm, hbm, hbm,
            hbm, hbm,
        ],
        out_specs=(vmem, vmem),
        scratch_shapes=[
            pltpu.VMEM((ROWS, 128), BF16),
            pltpu.VMEM((1, 128), F32),
            pltpu.VMEM((1, ROWS), jnp.int32),
            pltpu.VMEM((4, 32, 128), F32),
            pltpu.VMEM((4, 32, 128), BF16),
            pltpu.VMEM((4, 32, 128), BF16),
            pltpu.VMEM((2, 2, 32, 128), BF16),
            pltpu.VMEM((2, KEYS_DEV, 256), BF16),
            pltpu.VMEM((2, 2, 128, KEYS_DEV), BF16),
            pltpu.VMEM((2, 2, KEYS_DEV, 256), BF16),
            pltpu.VMEM((4, 2, 256, 128), BF16),
            pltpu.VMEM((4, 2, 256, 128), BF16),
            pltpu.VMEM((4, 2, 2, 8, 128), F32),
            pltpu.VMEM((16, 128, 128), BF16),
            pltpu.VMEM((16, 8, 128), F32),
            pltpu.VMEM((128, 128), F32),
            pltpu.VMEM((4, 4, 16, 1024), BF16),
            pltpu.VMEM((2048, 256), BF16),
            pltpu.VMEM((2, 128, 128), F32),
            pltpu.VMEM((128, 128), F32),
            pltpu.VMEM((4, 4, 2, 128, 128), BF16),
            pltpu.VMEM((8, 1, 128), F32),
            pltpu.VMEM((4, 1, 128), F32),
            pltpu.VMEM((D, VOCAB_DEV), BF16),
            pltpu.VMEM((ROWS, VOCAB_DEV), F32),
            pltpu.VMEM((32, 1, 384), F32),
            dma((8,)),
            dma((4,)),
            dma((3,)),
            dma((1,)),
            dma((1,)),
            dma((2, 4)),
            dma((2, 16)),
            dma((2,)),
            dma((2,)),
            dma((1,)),
            dma((1,)),
            dma((2, 4)),
            dma((2, 16)),
            dma((16,)),
            dma((2,)),
            dma((1,)),
            dma((14,)),
        ],
        compiler_params=pltpu.CompilerParams(
            collective_id=0, has_side_effects=True, vmem_limit_bytes=56 * 1024 * 1024
        ),
        name="score_response",
    )(
        queries, response_keys, response_values, prompt_keys, prompt_values, resp_len, residual,
        out_weight, norm_gain.reshape(1, 128), vocab_weight, targets.reshape(1, ROWS),
    )
    layer_out, row_loss = pl.pallas_call(
        hand_over, out_shape=shapes, in_specs=[vmem, vmem], out_specs=(vmem, vmem), name="hand_over"
    )(*results)
    return layer_out, row_loss.reshape(ROWS)


def solution(mesh):
    placed = (
        P(("batch", "seq"), None),
        P(("batch", "seq"), None),
        P(("batch", "seq"), None),
        P(("batch", "seq"), None),
        P(("batch", "seq"), None),
        P("batch"),
        P("batch", "seq"),
        P(None, "seq"),
        P("seq"),
        P(None, "seq"),
        P("batch"),
    )
    return jax.shard_map(
        local,
        mesh=mesh,
        in_specs=placed,
        out_specs=(P("batch", "seq"), P("batch")),
        check_vma=False,
    )
```

```python
import functools

import jax
import jax.numpy as jnp
from jax import lax
from jax.experimental import pallas as pl
from jax.experimental.pallas import tpu as pltpu
from jax.sharding import PartitionSpec as P

D = 4096
KEY_VALUE_HEADS = 4
HEAD_SIZE = 128
ROWS = 128
VOCAB_DEV = 2432
KEYS_DEV = 1024
LOG2E = 1.4426950408889634
SCORE_SCALE = LOG2E * HEAD_SIZE ** (-0.5)
MESH = pl.DeviceIdType.MESH
F32 = jnp.float32
BF16 = jnp.bfloat16


def dot_nt(a, b):
    return lax.dot_general(a, b, (((1,), (1,)), ((), ())), preferred_element_type=F32)


def dot_nn(a, b):
    return jnp.dot(a, b, preferred_element_type=F32)


def eye_mask():
    return lax.broadcasted_iota(jnp.int32, (128, 128), 0) == lax.broadcasted_iota(
        jnp.int32, (128, 128), 1
    )


def to_row(column):
    return jnp.sum(jnp.where(eye_mask(), column, 0.0), axis=0, keepdims=True)


def to_column(row):
    return jnp.sum(jnp.where(eye_mask(), row, 0.0), axis=1, keepdims=True)


def drain(ref, sem):
    pltpu.make_async_copy(ref, ref, sem).wait()


def kernel(
    queries, response_keys, response_values, prompt_keys, prompt_values, length, residual_in,
    out_weight, gain_in, vocab_weight, targets_in,
    layer_out, row_loss,
    residual, gain, targets, spread, small, resp, respbuf, kbuf, kt, vbuf, qbuf, ostage, sstage, rbuf, rstat, mrg, abuf, wbuf,
    pown, ppart, gbuf, ssbuf, ssplane, wv, acc, fbuf,
    local_sem, vocab_sem, kv_recv, w_recv, small_recv, q_ring, q_diag, r_recv, own_sem, a_recv,
    p_recv, g_ring, g_diag, h_recv, s_recv, f_recv, send_sem,
):
    me = lax.axis_index("seq")
    z, x, c = me // 8, (me // 2) % 4, me % 2
    chip = me // 2
    other = 1 - c
    sibling = chip * 2 + other

    def turn(a, d):
        return lax.rem(a + d, 4)

    def device(cz, cx, core):
        return (cz * 4 + cx) * 2 + core

    def send(src, dst, sem, target, kind):
        pltpu.make_async_remote_copy(
            src_ref=src, dst_ref=dst, send_sem=send_sem.at[kind], recv_sem=sem,
            device_id={"seq": target}, device_id_type=MESH,
        ).start()

    my_cols = pl.ds(pl.multiple_of(c * 256, 256), 256)
    other_cols = pl.ds(pl.multiple_of(other * 256, 256), 256)
    my_half = pl.ds(pl.multiple_of(c * 2048, 2048), 2048)
    other_half = pl.ds(pl.multiple_of(other * 2048, 2048), 2048)
    w_lane = pl.ds(pl.multiple_of(c * 128, 128), 128)

    barrier = pltpu.get_barrier_semaphore()
    x_peers = [device(z, turn(x, d), core) for d in (2, 1, 3) for core in (c, other)]
    z_peers = [device(turn(z, d), x, core) for d in (2, 1, 3) for core in (c, other)]
    for peer in z_peers + x_peers + [sibling]:
        pl.semaphore_signal(barrier, inc=1, device_id={"seq": peer}, device_id_type=MESH)

    own_copies = [
        pltpu.make_async_copy(prompt_keys.at[:, my_cols], kbuf.at[c], local_sem.at[0]),
        pltpu.make_async_copy(out_weight.at[my_half, :], wbuf.at[:, w_lane], local_sem.at[1]),
        pltpu.make_async_copy(residual_in, residual, local_sem.at[3]),
        pltpu.make_async_copy(gain_in, gain, local_sem.at[4]),
        pltpu.make_async_copy(targets_in, targets, local_sem.at[5]),
    ]
    value_copies = [
        pltpu.make_async_copy(
            prompt_values.at[:, pl.ds(pl.multiple_of(c * 256 + j * 128, 128), 128)],
            vbuf.at[j, c, :, pl.ds(0, 128)], local_sem.at[6 + j],
        )
        for j in range(2)
    ]
    for copy in own_copies + value_copies:
        copy.start()
    vbuf[:, :, :, 128:] = jnp.ones((2, 2, KEYS_DEV, 128), BF16)
    vocab_copies = [
        pltpu.make_async_copy(
            vocab_weight.at[pl.ds(i * 1024, 1024), :], wv.at[pl.ds(i * 1024, 1024), :],
            vocab_sem.at[i],
        )
        for i in range(4)
    ]

    wide = queries[...].astype(F32)
    for head in range(32):
        spread[head // 8, pl.ds(head % 8, 4, stride=8), :] = wide[:, head * 128 : head * 128 + 128]
    nothing = jnp.zeros((12, 128), F32)
    for g in range(4):
        cols = slice(g * 128, g * 128 + 128)
        small[g] = spread[g].astype(BF16)
        resp[g, 0:16, :] = jnp.concatenate([response_keys[:, cols].astype(F32), nothing], 0).astype(BF16)
        resp[g, 16:32, :] = jnp.concatenate([response_values[:, cols].astype(F32), nothing], 0).astype(BF16)
    q_rows = pl.ds(pl.multiple_of((x * 2 + c) * 32, 32), 32)
    my_heads, other_heads = pl.ds(2 * c, 2), pl.ds(2 * other, 2)
    for j in range(2):
        qbuf[z, j, q_rows, :] = small[2 * c + j]
        respbuf[c, j] = resp[2 * c + j]

    pl.semaphore_wait(barrier, 13)

    send(resp.at[other_heads], respbuf.at[c], small_recv.at[0], sibling, 1)
    def q_half(cz, cx, part):
        return qbuf.at[cz, part, pl.ds(pl.multiple_of(cx * 64, 64), 64), :]

    mine = qbuf.at[z, :, q_rows, :]
    send(small.at[other_heads], mine, q_ring.at[0, 0], sibling, 0)
    for d in (1, 3, 2):
        for core in (c, other):
            heads = small.at[pl.ds(2 * core, 2)]
            send(heads, mine, q_ring.at[0, 4 - d], device(z, turn(x, d), core), 0)
            send(heads, mine, q_ring.at[1, 4 - d], device(turn(z, d), x, core), 0)
    send(prompt_keys.at[:, other_cols], kbuf.at[c], kv_recv.at[0], sibling, 2)
    for j in range(2):
        send(
            prompt_values.at[:, pl.ds(pl.multiple_of(other * 256 + j * 128, 128), 128)],
            vbuf.at[j, c, :, pl.ds(0, 128)], kv_recv.at[1 + j], sibling, 2,
        )

    def turn_keys(core):
        for j in range(2):
            kt[j, core] = kbuf[core, :, j * 128 : (j + 1) * 128].T

    own_copies[0].wait()
    turn_keys(c)
    drain(kbuf.at[0], kv_recv.at[0])
    turn_keys(other)
    for d in (1, 3, 2):
        sx, sz = turn(x, d), turn(z, d)
        drain(qbuf.at[0, 0, pl.ds(0, 128), :], q_ring.at[0, d])
        for e in (1, 3, 2):
            block = q_half(z, sx, 0)
            send(block, block, q_diag.at[0, (4 - e) * 4 + d], device(turn(z, e), x, c), 12)
        drain(qbuf.at[0, 0, pl.ds(0, 128), :], q_ring.at[1, d])
        for e in (1, 3, 2):
            block = q_half(sz, x, 1)
            send(block, block, q_diag.at[1, d * 4 + 4 - e], device(z, turn(x, e), c), 12)
    drain(qbuf.at[0, 0, pl.ds(0, 64), :], q_ring.at[0, 0])
    send(out_weight.at[other_half, :], wbuf.at[:, w_lane], w_recv.at[0], sibling, 3)
    for copy in vocab_copies:
        copy.start()

    live = length[0]
    key_column = lax.broadcasted_iota(jnp.int32, (256, 32), 1)
    key_id = chip * 8 + (key_column // 16) * 4 + key_column % 16
    key_ok = (key_column % 16 < 4) & (key_id < live)
    row_in_plane = lax.broadcasted_iota(jnp.int32, (256, 32), 0) // 8
    drain(resp.at[pl.ds(0, 2)], small_recv.at[0])
    for j in range(2):
        value_copies[j].wait()
        drain(vbuf.at[0, 0, :, pl.ds(0, 128)], kv_recv.at[1 + j])

    def with_ones(v):
        return jnp.concatenate([v, jnp.ones_like(v)], 1)

    for u, offset in enumerate((0, 1 + 2 * (x % 2), 2, 3 - 2 * (x % 2))):
        t = turn(z, offset)
        if u > 0:
            for dx in (1, 3, 2):
                for part in range(2):
                    drain(qbuf.at[0, 0, pl.ds(0, 64), :], q_diag.at[part, offset * 4 + dx])

        visible = key_ok & (key_id <= t * 32 + row_in_plane)
        for j in range(2):
            q = qbuf[t, j]
            s0 = dot_nn(q, kt[j, 0])
            s1 = dot_nn(q, kt[j, 1])
            resp_keys = jnp.concatenate([respbuf[0, j, 0:16, :], respbuf[1, j, 0:16, :]], 0)
            resp_values = jnp.concatenate([respbuf[0, j, 16:32, :], respbuf[1, j, 16:32, :]], 0)
            sr = jnp.where(visible, dot_nt(q, resp_keys), -jnp.inf)
            peak = jnp.maximum(
                jnp.maximum(jnp.max(s0, 1, keepdims=True), jnp.max(s1, 1, keepdims=True)),
                jnp.max(sr, 1, keepdims=True),
            ) * SCORE_SCALE
            p0 = jnp.exp2(s0 * SCORE_SCALE - peak)
            p1 = jnp.exp2(s1 * SCORE_SCALE - peak)
            pr = jnp.exp2(sr * SCORE_SCALE - peak)
            o = (
                dot_nn(p0.astype(BF16), vbuf[j, 0])
                + dot_nn(p1.astype(BF16), vbuf[j, 1])
                + dot_nn(pr.astype(BF16), with_ones(resp_values))
            )
            total = o[:, 128:]
            ostage[u, j] = o[:, :128].astype(BF16)
            for half in range(2):
                rows = slice(half * 128, (half + 1) * 128)
                sstage[u, j, half, 0:1, :] = to_row(peak[rows])
                sstage[u, j, half, 1:2, :] = to_row(total[rows])
        for quarter in range(4):
            half, j = quarter // 2, quarter % 2
            owner = device(t, quarter, c)
            part = ostage.at[u, j, pl.ds(half * 128, 128), :]
            stat = sstage.at[u, j, half]

            def to_owner():
                send(part, rbuf.at[chip], r_recv.at[0], owner, 4)
                send(stat, rstat.at[chip], r_recv.at[1], owner, 5)

            if u > 0:
                to_owner()
                continue
            pl.when(owner != me)(to_owner)

            @pl.when(owner == me)
            def _():
                pltpu.make_async_copy(part, rbuf.at[chip], own_sem.at[0]).start()
                pltpu.make_async_copy(stat, rstat.at[chip], own_sem.at[1]).start()

    drain(rstat.at[pl.ds(0, 15)], r_recv.at[1])
    drain(rstat.at[0], own_sem.at[1])
    peaks = rstat[:, 0, :]
    weight = jnp.exp2(peaks - jnp.max(peaks, 0, keepdims=True))
    weight = weight / jnp.sum(weight * rstat[:, 1, :], 0, keepdims=True)
    weight = jnp.concatenate([weight, jnp.zeros((112, 128), F32)], 0).T
    drain(rbuf.at[pl.ds(0, 15)], r_recv.at[0])
    drain(rbuf.at[0], own_sem.at[0])
    merged = weight[:, 0:1] * rbuf[0].astype(F32)
    for k in range(1, 16):
        merged += weight[:, k : k + 1] * rbuf[k].astype(F32)
    mrg[...] = merged
    block = jnp.concatenate([mrg[pl.ds(h, 16, stride=8), :] for h in range(8)], 1)
    abuf[z, x] = block.astype(BF16)

    def torus_distance(d):
        return min(d[0], 4 - d[0]) + min(d[1], 4 - d[1])

    far_first = sorted([(dz, dx) for dz in range(4) for dx in range(4)], key=lambda d: -torus_distance(d))
    for dz, dx in far_first[:-1]:
        send(abuf.at[z, x], abuf.at[z, x], a_recv.at[0], device(turn(z, dz), turn(x, dx), c), 6)
    for copy in own_copies[1:]:
        copy.wait()
    drain(wbuf.at[:, pl.ds(0, 128)], w_recv.at[0])
    drain(rbuf.at[pl.ds(0, 15)], a_recv.at[0])
    attn = [
        jnp.concatenate([abuf[t, 2 * half + j] for t in range(4) for half in range(2)], 0)
        for j in range(2)
    ]

    def project(columns):
        lanes = pl.ds(pl.multiple_of(columns * 128, 128), 128)
        return dot_nn(attn[0], wbuf[pl.ds(0, 1024), lanes]) + dot_nn(
            attn[1], wbuf[pl.ds(1024, 1024), lanes]
        )

    pown[other] = project(other)
    send(pown.at[other], ppart, p_recv.at[0], sibling, 7)
    pown[c] = project(c)
    base = residual[...].astype(F32) + pown[c]
    drain(ppart, p_recv.at[0])
    layer = (base + ppart[...]).astype(BF16)
    layer_out[...] = layer
    layer = layer.astype(F32)
    gbuf[z, x, c] = (layer * gain[...]).astype(BF16)
    ssbuf[x * 2 + c] = to_row(jnp.sum(layer * layer, 1, keepdims=True))

    def gather(full, half, ring, diag, kind, first_sent, on_ring):
        for d in (1, 3, 2):
            send(full(z, x), full(z, x), ring.at[0, 4 - d], device(z, turn(x, d), c), kind)
            send(full(z, x), full(z, x), ring.at[1, 4 - d], device(turn(z, d), x, c), kind)
        first_sent()
        for d in (1, 3, 2):
            sx, sz = turn(x, d), turn(z, d)
            drain(full(0, 0), ring.at[0, d])
            for e in (1, 3, 2):
                block = half(z, sx, 0)
                send(block, block, diag.at[0, (4 - e) * 4 + d], device(turn(z, e), x, c), kind)
            on_ring(z, sx, d)
            drain(full(0, 0), ring.at[1, d])
            for e in (1, 3, 2):
                block = half(sz, x, 1)
                send(block, block, diag.at[1, d * 4 + 4 - e], device(z, turn(x, e), c), kind)
            on_ring(sz, x, d * 4)

    def g_full(cz, cx):
        return gbuf.at[cz, cx, c]

    def g_half(cz, cx, part):
        return gbuf.at[cz, cx, c, pl.ds(part * 64, 64), :]

    def to_sibling(cz, cx, index):
        send(g_full(cz, cx), g_full(cz, cx), h_recv.at[index], sibling, 9)

    def first_sent():
        to_sibling(z, x, 0)
        for peer in x_peers + [sibling]:
            mine = ssbuf.at[x * 2 + c]
            send(mine, mine, s_recv.at[0], peer, 10)

    gather(g_full, g_half, g_ring, g_diag, 8, first_sent, to_sibling)
    drain(ssbuf.at[pl.ds(0, 7)], s_recv.at[0])
    ssplane[z] = jnp.sum(ssbuf[:, 0, :], 0, keepdims=True)
    for d in (2, 1, 3):
        send(ssplane.at[z], ssplane.at[z], s_recv.at[1], device(turn(z, d), x, c), 11)

    def plane_features(cz):
        return jnp.concatenate([gbuf[cz, cx, core] for cx in range(4) for core in range(2)], 1)

    def plane_rows(cz):
        return pl.ds(pl.multiple_of(cz * 1024, 1024), 1024)

    for copy in vocab_copies:
        copy.wait()
    for dx in range(4):
        drain(gbuf.at[0, 0, 0], h_recv.at[dx])
    acc[...] = dot_nn(plane_features(z), wv[plane_rows(z), :])
    for dz in (1, 3, 2):
        for dx in (1, 3, 2):
            for part in range(2):
                drain(g_half(0, 0, part), g_diag.at[part, dz * 4 + dx])
            to_sibling(turn(z, dz), turn(x, dx), dz * 4 + dx)
    for dz in (1, 3, 2):
        for dx in range(4):
            drain(gbuf.at[0, 0, 0], h_recv.at[dz * 4 + dx])
    planes = [turn(z, dz) for dz in (1, 2, 3)]
    features = [plane_features(cz) for cz in planes]
    for n in range(0, VOCAB_DEV, 512):
        cols = slice(n, min(n + 512, VOCAB_DEV))
        part = acc[:, cols]
        for cz, f in zip(planes, features):
            part += dot_nn(f, wv[plane_rows(cz), cols])
        acc[:, cols] = part

    drain(ssplane.at[pl.ds(0, 3)], s_recv.at[1])
    squares = jnp.sum(ssplane[:, 0, :], 0, keepdims=True)
    inverse = to_column(lax.rsqrt(squares / D + 1e-06))
    logits = acc[...] * inverse
    top = jnp.max(logits, 1, keepdims=True)
    exp_total = jnp.sum(jnp.exp(logits - top), 1, keepdims=True)
    target = to_column(targets[...].astype(F32)).astype(jnp.int32) - me * VOCAB_DEV
    hit = lax.broadcasted_iota(jnp.int32, (ROWS, VOCAB_DEV), 1) == target
    target_logit = jnp.sum(jnp.where(hit, logits, 0.0), 1, keepdims=True)
    fbuf[me] = jnp.concatenate([to_row(top), to_row(exp_total), to_row(target_logit)], 1)

    for dz, dx in far_first:
        for core in (c, other):
            if (dz, dx) != (0, 0) or core is other:
                target_device = device(turn(z, dz), turn(x, dx), core)
                send(fbuf.at[me], fbuf.at[me], f_recv.at[0], target_device, 13)
    drain(fbuf.at[pl.ds(0, 31)], f_recv.at[0])
    tops = fbuf[:, 0, 0:128]
    top = jnp.max(tops, 0, keepdims=True)
    whole = jnp.sum(fbuf[:, 0, 128:256] * jnp.exp(tops - top), 0, keepdims=True)
    loss = top + jnp.log(whole) - jnp.sum(fbuf[:, 0, 256:384], 0, keepdims=True)
    row_ids = lax.broadcasted_iota(jnp.int32, (1, ROWS), 1)
    row_loss[...] = jnp.where(row_ids < live, loss, 0.0)

    drain(kbuf.at[0, pl.ds(0, 416), :], send_sem.at[0])
    drain(resp.at[pl.ds(0, 2)], send_sem.at[1])
    drain(kbuf, send_sem.at[2])
    drain(wbuf.at[:, pl.ds(0, 128)], send_sem.at[3])
    drain(rbuf.at[pl.ds(0, 15)], send_sem.at[4])
    drain(rstat.at[pl.ds(0, 15)], send_sem.at[5])
    drain(rbuf.at[pl.ds(0, 15)], send_sem.at[6])
    drain(ppart, send_sem.at[7])
    drain(rbuf.at[pl.ds(0, 15)], send_sem.at[8])
    drain(rbuf, send_sem.at[9])
    drain(ssbuf.at[pl.ds(0, 7)], send_sem.at[10])
    drain(ssplane.at[pl.ds(0, 3)], send_sem.at[11])
    drain(kbuf.at[0, pl.ds(0, 576), :], send_sem.at[12])
    drain(fbuf.at[pl.ds(0, 31)], send_sem.at[13])


def hand_over(layer, loss, layer_out, loss_out):
    layer_out[...] = layer[...]
    loss_out[...] = loss[...]


def local(
    queries, prompt_keys, prompt_values, response_keys, response_values, resp_len, residual,
    out_weight, norm_gain, vocab_weight, targets,
):
    vmem = pl.BlockSpec(memory_space=pltpu.VMEM)
    hbm = pl.BlockSpec(memory_space=pl.ANY)
    dma = pltpu.SemaphoreType.DMA
    shapes = (
        jax.ShapeDtypeStruct((ROWS, 128), BF16),
        jax.ShapeDtypeStruct((1, ROWS), F32),
    )
    results = pl.pallas_call(
        kernel,
        out_shape=shapes,
        in_specs=[
            vmem, vmem, vmem, hbm, hbm, pl.BlockSpec(memory_space=pltpu.SMEM), hbm, hbm, hbm,
            hbm, hbm,
        ],
        out_specs=(vmem, vmem),
        scratch_shapes=[
            pltpu.VMEM((ROWS, 128), BF16),
            pltpu.VMEM((1, 128), F32),
            pltpu.VMEM((1, ROWS), jnp.int32),
            pltpu.VMEM((4, 32, 128), F32),
            pltpu.VMEM((4, 32, 128), BF16),
            pltpu.VMEM((4, 32, 128), BF16),
            pltpu.VMEM((2, 2, 32, 128), BF16),
            pltpu.VMEM((2, KEYS_DEV, 256), BF16),
            pltpu.VMEM((2, 2, 128, KEYS_DEV), BF16),
            pltpu.VMEM((2, 2, KEYS_DEV, 256), BF16),
            pltpu.VMEM((4, 2, 256, 128), BF16),
            pltpu.VMEM((4, 2, 256, 128), BF16),
            pltpu.VMEM((4, 2, 2, 8, 128), F32),
            pltpu.VMEM((16, 128, 128), BF16),
            pltpu.VMEM((16, 8, 128), F32),
            pltpu.VMEM((128, 128), F32),
            pltpu.VMEM((4, 4, 16, 1024), BF16),
            pltpu.VMEM((2048, 256), BF16),
            pltpu.VMEM((2, 128, 128), F32),
            pltpu.VMEM((128, 128), F32),
            pltpu.VMEM((4, 4, 2, 128, 128), BF16),
            pltpu.VMEM((8, 1, 128), F32),
            pltpu.VMEM((4, 1, 128), F32),
            pltpu.VMEM((D, VOCAB_DEV), BF16),
            pltpu.VMEM((ROWS, VOCAB_DEV), F32),
            pltpu.VMEM((32, 1, 384), F32),
            dma((8,)),
            dma((4,)),
            dma((3,)),
            dma((1,)),
            dma((1,)),
            dma((2, 4)),
            dma((2, 16)),
            dma((2,)),
            dma((2,)),
            dma((1,)),
            dma((1,)),
            dma((2, 4)),
            dma((2, 16)),
            dma((16,)),
            dma((2,)),
            dma((1,)),
            dma((14,)),
        ],
        compiler_params=pltpu.CompilerParams(
            collective_id=0, has_side_effects=True, vmem_limit_bytes=56 * 1024 * 1024
        ),
        name="score_response",
    )(
        queries, response_keys, response_values, prompt_keys, prompt_values, resp_len, residual,
        out_weight, norm_gain.reshape(1, 128), vocab_weight, targets.reshape(1, ROWS),
    )
    layer_out, row_loss = pl.pallas_call(
        hand_over, out_shape=shapes, in_specs=[vmem, vmem], out_specs=(vmem, vmem), name="hand_over"
    )(*results)
    return layer_out, row_loss.reshape(ROWS)


def solution(mesh):
    placed = (
        P(("batch", "seq"), None),
        P(("batch", "seq"), None),
        P(("batch", "seq"), None),
        P(("batch", "seq"), None),
        P(("batch", "seq"), None),
        P("batch"),
        P("batch", "seq"),
        P(None, "seq"),
        P("seq"),
        P(None, "seq"),
        P("batch"),
    )
    return jax.shard_map(
        local,
        mesh=mesh,
        in_specs=placed,
        out_specs=(P("batch", "seq"), P("batch")),
        check_vma=False,
    )
```
